32 devices in a mesh: seq: 8 (over z, y), tp: 4 (over x, core).
Axes of the slice: x: 2, y: 2, z: 4, core: 2. Of those that a mesh axis runs over, the one named last changes fastest.
Arguments:
- tokens: bfloat16 [2048, 2048], P('seq', 'tp'), may hold values from -6 to 6
- norm_gain: float32 [2048], replicated, may hold values from 0.1 to 1.9
- w_query: bfloat16 [2048, 1024], P(None, 'tp'), may hold values from -0.125 to 0.125
- w_key: bfloat16 [2048, 1024], P(None, 'tp'), may hold values from -0.125 to 0.125
- w_value: bfloat16 [2048, 2048], P(None, 'tp'), may hold values from -0.125 to 0.125
- w_gate_out: bfloat16 [2048, 2048], P(None, 'tp'), may hold values from -0.125 to 0.125
- gate_down: bfloat16 [2048, 16], replicated, may hold values from -0.09272438 to 0.09272438
- gate_up: bfloat16 [16, 1024], P(None, 'tp'), may hold values from -1 to 1.2625
- gate_bias: float32 [1024], P('tp'), may hold values from 1 to 8
- head_gain: float32 [2048], P('tp'), may hold values from 0.1 to 1.9
- w_out: bfloat16 [2048, 2048], P('tp'), may hold values from -0.125 to 0.125
- request_ids: int32 [2048], P('seq'), may hold values from 0 to 3, as said below
Outputs:
- mixed: bfloat16 [2048, 2048], P('seq', 'tp')
The draws below stay inside these ranges and needn't reach their ends.
Inputs may be any that keep to these rules, and one draw needn't show every extreme that they name: `request_ids`: request numbers never fall along the tokens; every request of 0 to 3 holds 1 to 1024 tokens; request 0 holds fewer than 256 tokens and request 1 holds exactly 1024.
All inputs are finite; a program needn't handle non-finite values.
Results may differ from the reference program's by a relative error of at most 0.015.
Values may be sent and summed in bfloat16 or wider, within the bound.
A program may use at most 128 MiB of HBM per device.

```python
import jax
import jax.numpy as jnp
from jax import lax

D = 2048
H = 4
K = 256
V = 512
R = 16
C = 64
TOK_DEV = 256
TOKEN_COUNT = 2048
MAXLEN = 1024
REQUEST_COUNT = 4


def shared_direction(key):
    bits = jax.random.randint(jax.random.fold_in(key, 11), (D,), 0, 2, dtype=jnp.int32)
    return (2 * bits - 1).astype(jnp.float32)


def request_layout(key):
    others = REQUEST_COUNT - 2
    head_length = jax.random.randint(jax.random.fold_in(key, 24), (), 1, TOK_DEV, dtype=jnp.int32)
    first = jax.random.randint(jax.random.fold_in(key, 21), (others,), 1, 33, dtype=jnp.int32)
    second = jax.random.randint(jax.random.fold_in(key, 22), (others,), 1, 33, dtype=jnp.int32)
    shares = first * second
    spare = (MAXLEN - head_length - others).astype(jnp.int32)
    total = jnp.sum(shares).astype(jnp.int32)
    base = (spare * shares // total).astype(jnp.int32)
    rest = (spare - jnp.sum(base)).astype(jnp.int32)
    order = jnp.arange(others, dtype=jnp.int32)
    other_lengths = (1 + base + (order < rest).astype(jnp.int32)).astype(jnp.int32)
    index = jnp.arange(REQUEST_COUNT, dtype=jnp.int32)
    tail = other_lengths[jnp.clip(index - 2, 0, others - 1)]
    lengths = jnp.where(index == 0, head_length, jnp.where(index == 1, MAXLEN, tail)).astype(jnp.int32)
    ends = jnp.cumsum(lengths).astype(jnp.int32)
    position = jnp.arange(TOKEN_COUNT, dtype=jnp.int32)
    ids = jnp.sum((position[:, None] >= ends[None, :]).astype(jnp.int32), axis=1)
    return ids.astype(jnp.int32)


def request_lift(key, ids):
    chosen = jax.random.randint(jax.random.fold_in(key, 31), (REQUEST_COUNT,), 0, 2, dtype=jnp.int32).astype(jnp.float32)
    amount = jax.random.uniform(jax.random.fold_in(key, 33), (REQUEST_COUNT,), jnp.float32, 0.8, 1.2)
    return (chosen * amount)[ids]


def draw_request_ids(key, part):
    return request_layout(key)


def draw_tokens(key, part):
    ids = request_layout(key)
    lift = request_lift(key, ids)
    direction = shared_direction(key)
    noise_key = jax.random.fold_in(key, 41)
    noise = jax.random.truncated_normal(noise_key, -5.5, 5.5, (TOKEN_COUNT, D), jnp.float32)
    values = 0.98 * noise + 0.15 * lift[:, None] * direction[None, :]
    return values.astype(jnp.bfloat16)


def draw_gate_down(key, part):
    direction = shared_direction(key)
    noise = jax.random.truncated_normal(jax.random.fold_in(key, 51), -4.0, 4.0, (D, R), jnp.float32) * D ** (-0.5)
    return (noise + 7.0 / D * direction[:, None]).astype(jnp.bfloat16)


def draw_gate_up(key, part):
    noise = jax.random.truncated_normal(jax.random.fold_in(key, 61), -4.0, 4.0, (R, H * K), jnp.float32) * R ** (-0.5)
    lift = jax.random.uniform(jax.random.fold_in(key, 63), (H * K,), jnp.float32, 1.5, 4.0)
    return (noise + lift[None, :] / R).astype(jnp.bfloat16)


def draw_gate_bias(key, part):
    return jax.random.uniform(jax.random.fold_in(key, 71), (H * K,), jnp.float32, 1.0, 5.0)


def steps_of(own_key, shape, cuts, low, top_value):
    def one(dim, shards_of):
        draws = jax.random.uniform(jax.random.fold_in(jax.random.fold_in(own_key, 6), dim), (shards_of,), jnp.float32, low / len(cuts), top_value / len(cuts))
        return jnp.repeat(jnp.exp(draws), shape[dim] // shards_of).reshape((-1,) + (1,) * (len(shape) - dim - 1))

    level = one(*cuts[0])
    for cut in cuts[1:]:
        level = level * one(*cut)
    return level


def scatter_about(stream_key, dims, scale, limit, split=(), kind=jnp.bfloat16):
    values = scale * jax.random.normal(stream_key, dims, jnp.float32)
    if split:
        values = values * steps_of(stream_key, dims, split, -0.22, 0.18)
    return jnp.clip(values, -limit, limit).astype(kind)


def setup_inputs(seed: int = 0) -> dict:
    splits = jax.random.split(jax.random.key(seed), 13)
    return {
        "tokens": draw_tokens(jax.random.fold_in(splits[12], 71), 0),
        "norm_gain": jnp.clip(1.0 + 0.18 * jax.random.normal(splits[1], (D,), jnp.float32), 0.1, 1.9),
        "w_query": scatter_about(splits[2], (D, H * K), D ** -0.5, 0.125, ((1, 4),)),
        "w_key": scatter_about(splits[3], (D, H * K), D ** -0.5, 0.125, ((1, 4),)),
        "w_value": scatter_about(splits[4], (D, H * V), D ** -0.5, 0.125, ((1, 4),)),
        "w_gate_out": scatter_about(splits[5], (D, H * V), D ** -0.5, 0.125, ((1, 4),)),
        "gate_down": draw_gate_down(jax.random.fold_in(splits[12], 71), 0),
        "gate_up": draw_gate_up(jax.random.fold_in(splits[12], 71), 0),
        "gate_bias": draw_gate_bias(jax.random.fold_in(splits[12], 71), 0),
        "head_gain": jnp.clip(1.0 + 0.18 * jax.random.normal(splits[9], (H * V,), jnp.float32), 0.1, 1.9),
        "w_out": scatter_about(splits[10], (H * V, D), (H * V) ** -0.5, 0.125, ((0, 4),)),
        "request_ids": draw_request_ids(jax.random.fold_in(splits[12], 71), 0),
    }


def rms(value, gain):
    return value * lax.rsqrt(lax.optimization_barrier(jnp.mean(value * value, axis=-1, keepdims=True)) + 1e-05) * gain

def group_terms(query, key, value, log_decay_rate, ids, prev):
    cum = jnp.cumsum(log_decay_rate, axis=0)
    query_decayed = (query.astype(jnp.float32) * jnp.exp(cum) * K ** (-0.5)).astype(jnp.bfloat16)
    kinv = (key.astype(jnp.float32) * jnp.exp(-cum)).astype(jnp.bfloat16)
    scores = jnp.dot(query_decayed, kinv.T, preferred_element_type=jnp.float32)
    place = jnp.arange(query.shape[0], dtype=jnp.int32)
    allowed = (place[None, :] <= place[:, None]) & (ids[None, :] == ids[:, None])
    weights = jnp.where(allowed, scores, 0.0).astype(jnp.bfloat16)
    intra = jnp.dot(weights, value, preferred_element_type=jnp.float32)
    causal_mask = ids == prev
    keep = (ids == ids[-1]).astype(jnp.float32)[:, None]
    kend = (key.astype(jnp.float32) * jnp.exp(cum[-1:] - cum) * keep).astype(jnp.bfloat16)
    fresh = jnp.dot(kend.T, value, preferred_element_type=jnp.float32)
    decay = jnp.exp(cum[-1]) * (ids[-1] == prev).astype(jnp.float32)
    return (query_decayed, intra, causal_mask, fresh, decay)

def reference(tokens, norm_gain, w_query, w_key, w_value, w_gate_out, gate_down, gate_up, gate_bias, head_gain, w_out, request_ids):
    normed = rms(tokens.astype(jnp.float32), norm_gain).astype(jnp.bfloat16)
    low = jnp.dot(normed, gate_down, preferred_element_type=jnp.float32).astype(jnp.bfloat16)
    log_decay_rate = jax.nn.log_sigmoid(jnp.dot(low, gate_up, preferred_element_type=jnp.float32) + gate_bias) / 16.0
    query = jnp.dot(normed, w_query, preferred_element_type=jnp.float32).astype(jnp.bfloat16)
    key = jnp.dot(normed, w_key, preferred_element_type=jnp.float32).astype(jnp.bfloat16)
    value = jnp.dot(normed, w_value, preferred_element_type=jnp.float32).astype(jnp.bfloat16)
    opengate = jnp.dot(normed, w_gate_out, preferred_element_type=jnp.float32)
    blocks = TOKEN_COUNT // C
    request_id_block = request_ids.reshape(blocks, C)
    results = []
    for head in range(H):
        qh = query[:, head * K:(head + 1) * K].reshape(blocks, C, K)
        kh = key[:, head * K:(head + 1) * K].reshape(blocks, C, K)
        vh = value[:, head * V:(head + 1) * V].reshape(blocks, C, V)
        gh = log_decay_rate[:, head * K:(head + 1) * K].reshape(blocks, C, K)

        def step(carry, item):
            state, prev = carry
            qc, kc, vc, gc, sc = item
            query_decayed, intra, causal_mask, fresh, decay = group_terms(qc, kc, vc, gc, sc, prev)
            inter = jnp.dot(query_decayed.astype(jnp.float32), state, precision=lax.Precision.HIGHEST)
            attn = intra + jnp.where(causal_mask[:, None], inter, 0.0)
            return ((decay[:, None] * state + fresh, sc[-1]), attn)
        start = (jnp.zeros((K, V), jnp.float32), jnp.array(-1, jnp.int32))
        _, attn = lax.scan(step, start, (qh, kh, vh, gh, request_id_block))
        attn = attn.reshape(TOKEN_COUNT, V)
        gated = rms(attn, head_gain[head * V:(head + 1) * V]) * jax.nn.silu(opengate[:, head * V:(head + 1) * V])
        results.append(gated.astype(jnp.bfloat16))
    gated_all = jnp.concatenate(results, axis=1)
    return jnp.dot(gated_all, w_out, preferred_element_type=jnp.float32).astype(jnp.bfloat16)
```

```python
import functools

import jax
import jax.numpy as jnp
from jax import lax
from jax.experimental import pallas as pl
from jax.experimental.pallas import tpu as pltpu
from jax.sharding import PartitionSpec as P

K = 256
V = 512
C = 64
F32 = jnp.float32
BF16 = jnp.bfloat16
MESH = pl.DeviceIdType.MESH
TOKEN_CHUNKS = 4
STATE_CHUNKS = 4
OUT_CHUNKS = 2


def dot(a, b):
    return jnp.dot(a, b, preferred_element_type=F32)


def dot_nt(a, b):
    return lax.dot_general(a, b, (((1,), (1,)), ((), ())), preferred_element_type=F32)


def dot_tn(a, b):
    return lax.dot_general(a, b, (((0,), (0,)), ((), ())), preferred_element_type=F32)


def kernel(
    pairs,
    tokens_ref, gain_ref, wq_hbm, wk_hbm, wv_hbm, wg_hbm, down_ref, up_ref, bias_ref,
    head_gain_ref, wo_hbm, ids_ref,
    out_ref,
    tok, wq, wk, wv, wg, wo,
    acc_q, acc_k, acc_v, acc_g, acc_low, ssq_all,
    attn_ref, qin_ref, gated_ref,
    id_out, id_in, p_own, p_other,
    s_own, s_other, e_in, e_out, i_out, incoming,
    mate_out, mate_in, x_out, x_in, keep_x, keep_own,
    load_sem, tok_sem, tok_x, tok_x_in, tok_mate, tok_mate_in, tok_fwd, tok_fwd_in,
    id_sem, p_sem, s_sem, s_sem_in, e_sem, e_sem_in, i_sem, i_sem_in,
    m_sem, m_sem_in, x_sem, x_sem_in, ssq_sem, ssq_sem_in,
):
    s, t = lax.axis_index("seq"), lax.axis_index("tp")
    y, g = s % 2, s // 2
    rows, feats = tokens_ref.shape
    mate = t + 1 - 2 * (t % 2)
    across = (t + 2) % 4
    diagonal = (mate + 2) % 4
    partner = s + 1 - 2 * y
    last = pairs - 1

    def remote(src, dst, send, recv, where):
        return pltpu.make_async_remote_copy(
            src_ref=src, dst_ref=dst, send_sem=send, recv_sem=recv,
            device_id=where, device_id_type=MESH)

    own_tokens = pltpu.make_async_copy(tokens_ref, tok.at[t], tok_sem)
    own_tokens.start()
    loads = [
        pltpu.make_async_copy(src, dst, load_sem.at[i])
        for i, (src, dst) in enumerate([(wk_hbm, wk), (wv_hbm, wv), (wq_hbm, wq), (wg_hbm, wg)])
    ]
    loads += [
        pltpu.make_async_copy(wo_hbm.at[:, pl.ds(j * feats, feats)], wo.at[j], load_sem.at[4 + j])
        for j in range(4)
    ]
    for load in loads:
        load.start()

    barrier = pltpu.get_barrier_semaphore()
    up_g, down_g = (g + 1) % pairs, (g + last) % pairs
    skew = ((g + y * 2 - 1 + pairs) % pairs) * 2 + 1 - y
    for device in ((s, mate), (s, across), (s, diagonal), (partner, t), (up_g * 2 + y, t), (down_g * 2 + y, t), (skew, t)):
        pl.semaphore_signal(barrier, inc=1, device_id=device, device_id_type=MESH)
    id_row = ids_ref[...].astype(F32)
    id_last = id_row[:, rows - 1:rows]
    id_out[...] = jnp.broadcast_to(id_last, id_out.shape)
    acc_q[...] = jnp.zeros_like(acc_q)
    acc_k[...] = jnp.zeros_like(acc_k)
    acc_v[...] = jnp.zeros_like(acc_v)
    acc_g[...] = jnp.zeros_like(acc_g)
    acc_low[...] = jnp.zeros_like(acc_low)
    own_tokens.wait()
    own = tok[t].astype(F32)
    squares = jnp.sum(own * own, axis=-1, keepdims=True)
    ssq_all[0] = jnp.broadcast_to(squares, (rows, 128)).T[0:8]
    pl.semaphore_wait(barrier, 7)
    send_ssq = [
        remote(ssq_all.at[0], ssq_all.at[i + 1], ssq_sem.at[i], ssq_sem_in.at[i], (s, peer))
        for i, peer in enumerate((mate, across, diagonal))
    ]
    for copy in send_ssq:
        copy.start()

    size = rows // TOKEN_CHUNKS

    def piece(block, c):
        return tok.at[block, pl.ds(c * size, size)]

    to_x = [remote(piece(t, c), piece(t, c), tok_x.at[c], tok_x_in.at[c], (s, across)) for c in range(TOKEN_CHUNKS)]
    to_mate = [remote(piece(t, c), piece(t, c), tok_mate.at[c], tok_mate_in.at[c], (s, mate)) for c in range(TOKEN_CHUNKS)]
    from_x = [remote(piece(across, c), piece(across, c), tok_x.at[c], tok_x_in.at[c], (s, across)) for c in range(TOKEN_CHUNKS)]
    from_mate = [remote(piece(mate, c), piece(mate, c), tok_mate.at[c], tok_mate_in.at[c], (s, mate)) for c in range(TOKEN_CHUNKS)]
    forward = [remote(piece(across, c), piece(across, c), tok_fwd.at[c], tok_fwd_in.at[c], (s, mate)) for c in range(TOKEN_CHUNKS)]
    from_fwd = [remote(piece(diagonal, c), piece(diagonal, c), tok_fwd.at[c], tok_fwd_in.at[c], (s, mate)) for c in range(TOKEN_CHUNKS)]
    for c in range(TOKEN_CHUNKS):
        to_x[c].start()
        to_mate[c].start()

    send_id = remote(id_out, id_in, id_sem.at[0], id_sem.at[1], (s + 1, t))

    @pl.when(s < 2 * pairs - 1)
    def _():
        send_id.start()

    def project(block):
        xg = (tok[block].astype(F32) * r * gain_ref[block]).astype(BF16)
        acc_low[...] += dot_nt(xg, down_ref[:, pl.ds(pl.multiple_of(block * feats, feats), feats)])
        acc_k[...] += dot(xg, wk[block])
        acc_v[...] += dot(xg, wv[block])
        acc_q[...] += dot(xg, wq[block])
        acc_g[...] += dot(xg, wg[block])

    for copy in send_ssq:
        copy.wait_recv()
    total = ssq_all[0] + ssq_all[1] + ssq_all[2] + ssq_all[3]
    scale_row = lax.rsqrt(total / (4 * feats) + 1e-5)[0:1]
    r = jnp.broadcast_to(scale_row, (128, rows)).T[:, 0:1]
    for load in loads[:4]:
        load.wait()
    project(t)
    from_x[0].wait_recv()
    forward[0].start()
    for c in range(TOKEN_CHUNKS):
        from_mate[c].wait_recv()
    project(mate)
    for c in range(1, TOKEN_CHUNKS):
        from_x[c].wait_recv()
        forward[c].start()
    project(across)
    for c in range(TOKEN_CHUNKS):
        from_fwd[c].wait_recv()
    project(diagonal)

    low = acc_low[...].astype(BF16)
    z = dot(low, up_ref[...]) + bias_ref[...]
    rate = (jnp.minimum(z, 0.0) - jnp.log1p(jnp.exp(-jnp.abs(z)))) / 16.0
    row = lax.broadcasted_iota(jnp.int32, (rows, rows), 0)
    col = lax.broadcasted_iota(jnp.int32, (rows, rows), 1)
    within = jnp.where((row // C == col // C) & (col <= row), 1.0, 0.0).astype(BF16)
    high = rate.astype(BF16)
    rest = rate - high.astype(F32)
    middle = rest.astype(BF16)
    tiny = (rest - middle.astype(F32)).astype(BF16)
    cum = dot(within, high) + dot(within, middle) + dot(within, tiny)
    blocks = rows // C
    totals = [cum[(b + 1) * C - 1:(b + 1) * C] for b in range(blocks)]
    id_col = jnp.broadcast_to(id_row, (rows, rows)).T

    @pl.when(s == 0)
    def _():
        id_in[...] = jnp.full_like(id_in, -1.0)

    @pl.when(s > 0)
    def _():
        send_id.wait_recv()

    id_prev = id_in[0:1, 0:1]
    key = acc_k[...].astype(BF16).astype(F32)
    value = acc_v[...].astype(BF16)
    keep = jnp.where(id_col[:, 0:1] == id_last, 1.0, 0.0)
    zero = jnp.zeros_like(totals[0])
    kend, kdev = [], []
    for b in range(blocks):
        mine = slice(b * C, (b + 1) * C)
        end = key[mine] * jnp.exp(totals[b] - cum[mine])
        kend.append(end)
        kdev.append((end * jnp.exp(sum(totals[b + 1:], zero)) * keep[mine]).astype(BF16))
    state = dot_tn(value, jnp.concatenate(kdev, axis=0))
    s_own[...] = state.astype(BF16)
    going_on = jnp.where(id_last == id_prev, 1.0, 0.0)
    p_own[...] = jnp.broadcast_to(jnp.exp(sum(totals, zero)) * going_on, p_own.shape)

    half = V // 2
    span = half // STATE_CHUNKS

    def part(ref, owner, c):
        return ref.at[pl.ds(pl.multiple_of(owner * half + c * span, span), span)]

    def small(ref, c):
        return ref.at[pl.ds(c * span, span)]

    send_p = remote(p_own, p_other, p_sem.at[0], p_sem.at[1], (partner, t))
    send_p.start()
    swap = [remote(part(s_own, 1 - y, c), small(s_other, c), s_sem.at[c], s_sem_in.at[c], (partner, t)) for c in range(STATE_CHUNKS)]
    for c in range(STATE_CHUNKS):
        swap[c].start()
    chain = [remote(small(e_out, c), small(e_in, c), e_sem.at[c], e_sem_in.at[c], (s + 2, t)) for c in range(STATE_CHUNKS)]
    give = [remote(small(i_out, c), part(incoming, y, c), i_sem.at[c], i_sem_in.at[c], (partner, t)) for c in range(STATE_CHUNKS)]
    take = [remote(small(i_out, c), part(incoming, 1 - y, c), i_sem.at[c], i_sem_in.at[c], (partner, t)) for c in range(STATE_CHUNKS)]

    grow = jnp.exp(cum)
    query = acc_q[...].astype(BF16).astype(F32)
    qdec = (query * grow * K ** -0.5).astype(BF16)
    kinv = (key * jnp.exp(-cum)).astype(BF16)
    from_prev = jnp.where(id_col[:, 0:1] == id_prev, 1.0, 0.0)
    for b in range(blocks):
        mine = slice(b * C, (b + 1) * C)
        seen = (b + 1) * C
        keys = [
            (kend[a] * jnp.exp(sum(totals[a + 1:b], zero))).astype(BF16) for a in range(b)
        ] + [kinv[mine]]
        scores = dot_nt(qdec[mine], jnp.concatenate(keys, axis=0))
        allowed = (col[mine, :seen] <= row[mine, :seen]) & (id_col[mine, :seen] == id_row[:, :seen])
        weights = jnp.where(allowed, scores, 0.0).astype(BF16)
        attn_ref[mine, :] = dot(weights, value[:seen])
        qin_ref[mine, :] = (
            qdec[mine].astype(F32) * jnp.exp(sum(totals[:b], zero)) * from_prev[mine]
        ).astype(BF16)

    @pl.when(g == 0)
    def _():
        e_in[...] = jnp.zeros_like(e_in)

    second = y.astype(F32)
    first = 1.0 - second
    send_p.wait_recv()
    own_decay, other_decay = p_own[0:1, :], p_other[0:1, :]
    p0 = own_decay * first + other_decay * second
    p1 = own_decay * second + other_decay * first
    for c in range(STATE_CHUNKS):
        swap[c].wait_recv()
        mine = pl.ds(c * span, span)
        place = pl.ds(pl.multiple_of(y * half + c * span, span), span)
        a, b = s_own[place, :].astype(F32), s_other[mine, :].astype(F32)
        s0 = a * first + b * second
        s1 = a * second + b * first

        @pl.when(g > 0)
        def _():
            chain[c].wait_recv()

        entry = e_in[mine, :].astype(F32)
        middle_state = p0 * entry + s0
        e_out[mine, :] = (p1 * middle_state + s1).astype(BF16)

        @pl.when(g < last)
        def _():
            chain[c].start()

        i_out[mine, :] = (middle_state * first + entry * second).astype(BF16)
        give[c].start()
        incoming[place, :] = (entry * first + middle_state * second).astype(BF16)
    for c in range(STATE_CHUNKS):
        take[c].wait_recv()

    attn = attn_ref[...] + dot_nt(qin_ref[...], incoming[...])
    scale = lax.rsqrt(jnp.mean(attn * attn, axis=-1, keepdims=True) + 1e-5)
    opengate = acc_g[...]
    gated_ref[...] = (attn * scale * head_gain_ref[...] * (opengate * jax.nn.sigmoid(opengate))).astype(BF16)
    for load in loads[4:]:
        load.wait()
    lot = rows // OUT_CHUNKS

    def lines(c):
        return pl.ds(c * lot, lot)

    share = [
        [remote(mate_out.at[k, lines(c)], mate_in.at[k, lines(c)], m_sem.at[k, c], m_sem_in.at[k, c], (s, mate)) for c in range(OUT_CHUNKS)]
        for k in range(2)
    ]
    over = [remote(x_out.at[lines(c)], x_in.at[lines(c)], x_sem.at[c], x_sem_in.at[c], (s, across)) for c in range(OUT_CHUNKS)]
    for c in range(OUT_CHUNKS):
        mate_out[0, lines(c), :] = dot(gated_ref[lines(c), :], wo[diagonal]).astype(BF16)
        share[0][c].start()
        keep_x[lines(c), :] = dot(gated_ref[lines(c), :], wo[across])
    for c in range(OUT_CHUNKS):
        share[0][c].wait_recv()
        x_out[lines(c), :] = (keep_x[lines(c), :] + mate_in[0, lines(c), :].astype(F32)).astype(BF16)
        over[c].start()
    for c in range(OUT_CHUNKS):
        mate_out[1, lines(c), :] = dot(gated_ref[lines(c), :], wo[mate]).astype(BF16)
        share[1][c].start()
        keep_own[lines(c), :] = dot(gated_ref[lines(c), :], wo[t])
    for c in range(OUT_CHUNKS):
        share[1][c].wait_recv()
        over[c].wait_recv()
        out_ref[lines(c), :] = (
            keep_own[lines(c), :] + mate_in[1, lines(c), :].astype(F32) + x_in[lines(c), :].astype(F32)
        ).astype(BF16)

    for copy in to_x + to_mate + forward + send_ssq + [send_p] + swap + give + share[0] + share[1] + over:
        copy.wait_send()

    @pl.when(s < 2 * pairs - 1)
    def _():
        send_id.wait_send()

    @pl.when(g < last)
    def _():
        for c in range(STATE_CHUNKS):
            chain[c].wait_send()


def per_device(
    pairs,
    tokens, norm_gain, w_query, w_key, w_value, w_gate_out, gate_down, gate_up, gate_bias,
    head_gain, w_out, request_ids,
):
    rows, feats = tokens.shape
    ranks = gate_down.shape[1]
    vmem = pl.BlockSpec(memory_space=pltpu.VMEM)
    hbm = pl.BlockSpec(memory_space=pl.ANY)
    half = V // 2
    dma = pltpu.SemaphoreType.DMA
    scratch = [
        pltpu.VMEM((4, rows, feats), BF16),
        pltpu.VMEM((4, feats, K), BF16),
        pltpu.VMEM((4, feats, K), BF16),
        pltpu.VMEM((4, feats, V), BF16),
        pltpu.VMEM((4, feats, V), BF16),
        pltpu.VMEM((4, V, feats), BF16),
        pltpu.VMEM((rows, K), F32),
        pltpu.VMEM((rows, K), F32),
        pltpu.VMEM((rows, V), F32),
        pltpu.VMEM((rows, V), F32),
        pltpu.VMEM((rows, ranks), F32),
        pltpu.VMEM((4, 8, rows), F32),
        pltpu.VMEM((rows, V), F32),
        pltpu.VMEM((rows, K), BF16),
        pltpu.VMEM((rows, V), BF16),
        pltpu.VMEM((8, 128), F32),
        pltpu.VMEM((8, 128), F32),
        pltpu.VMEM((8, K), F32),
        pltpu.VMEM((8, K), F32),
        pltpu.VMEM((V, K), BF16),
        pltpu.VMEM((half, K), BF16),
        pltpu.VMEM((half, K), BF16),
        pltpu.VMEM((half, K), BF16),
        pltpu.VMEM((half, K), BF16),
        pltpu.VMEM((V, K), BF16),
        pltpu.VMEM((2, rows, feats), BF16),
        pltpu.VMEM((2, rows, feats), BF16),
        pltpu.VMEM((rows, feats), BF16),
        pltpu.VMEM((rows, feats), BF16),
        pltpu.VMEM((rows, feats), F32),
        pltpu.VMEM((rows, feats), F32),
        dma((8,)),
        dma,
        dma((TOKEN_CHUNKS,)), dma((TOKEN_CHUNKS,)),
        dma((TOKEN_CHUNKS,)), dma((TOKEN_CHUNKS,)),
        dma((TOKEN_CHUNKS,)), dma((TOKEN_CHUNKS,)),
        dma((2,)), dma((2,)),
        dma((STATE_CHUNKS,)), dma((STATE_CHUNKS,)),
        dma((STATE_CHUNKS,)), dma((STATE_CHUNKS,)),
        dma((STATE_CHUNKS,)), dma((STATE_CHUNKS,)),
        dma((2, OUT_CHUNKS)), dma((2, OUT_CHUNKS)),
        dma((OUT_CHUNKS,)), dma((OUT_CHUNKS,)),
        dma((3,)), dma((3,)),
    ]
    return pl.pallas_call(
        functools.partial(kernel, pairs),
        out_shape=jax.ShapeDtypeStruct((rows, feats), BF16),
        in_specs=[hbm, vmem, hbm, hbm, hbm, hbm, vmem, vmem, vmem, vmem, hbm, vmem],
        out_specs=vmem,
        scratch_shapes=scratch,
        compiler_params=pltpu.CompilerParams(
            collective_id=0, has_side_effects=True, vmem_limit_bytes=62 * 2**20),
        cost_estimate=pl.CostEstimate(flops=2_500_000_000, bytes_accessed=10_000_000, transcendentals=400_000),
        name="gla",
    )(
        tokens,
        norm_gain.reshape(4, 1, feats),
        w_query.reshape(4, feats, K),
        w_key.reshape(4, feats, K),
        w_value.reshape(4, feats, V),
        w_gate_out.reshape(4, feats, V),
        gate_down.T,
        gate_up,
        gate_bias.reshape(1, K),
        head_gain.reshape(1, V),
        w_out,
        request_ids.reshape(1, rows),
    )


def solution(mesh):
    return jax.shard_map(
        functools.partial(per_device, mesh.shape["seq"] // 2),
        mesh=mesh,
        in_specs=(
            P("seq", "tp"),
            P(),
            P(None, "tp"),
            P(None, "tp"),
            P(None, "tp"),
            P(None, "tp"),
            P(),
            P(None, "tp"),
            P("tp"),
            P("tp"),
            P("tp", None),
            P("seq"),
        ),
        out_specs=P("seq", "tp"),
        check_vma=False,
    )
```

```python
import functools

import jax
import jax.numpy as jnp
from jax import lax
from jax.experimental import pallas as pl
from jax.experimental.pallas import tpu as pltpu
from jax.sharding import PartitionSpec as P

K = 256
V = 512
C = 64
F32 = jnp.float32
BF16 = jnp.bfloat16
MESH = pl.DeviceIdType.MESH
TOKEN_CHUNKS = 4
STATE_CHUNKS = 4
OUT_CHUNKS = 4


def dot(a, b):
    return jnp.dot(a, b, preferred_element_type=F32)


def dot_nt(a, b):
    return lax.dot_general(a, b, (((1,), (1,)), ((), ())), preferred_element_type=F32)


def dot_tn(a, b):
    return lax.dot_general(a, b, (((0,), (0,)), ((), ())), preferred_element_type=F32)


def kernel(
    pairs,
    tokens_ref, gain_ref, wq_hbm, wk_hbm, wv_hbm, wg_hbm, down_ref, up_ref, bias_ref,
    head_gain_ref, wo_hbm, ids_ref,
    out_ref,
    tok, wq, wk, wv, wg, wo,
    acc_q, acc_k, acc_v, acc_g, acc_low, ssq_all,
    attn_ref, qin_ref, gated_ref,
    id_out, id_in, p_own, p_other,
    s_own, s_other, e_in, e_out, i_out, incoming,
    mate_out, mate_in, x_out, x_in, keep_x, keep_own, pair_first, pair_state,
    load_sem, tok_sem, tok_x, tok_x_in, tok_mate, tok_mate_in, tok_fwd, tok_fwd_in,
    id_sem, p_sem, s_sem, s_sem_in, e_sem, e_sem_in, i_sem, i_sem_in,
    m_sem, m_sem_in, x_sem, x_sem_in, ssq_sem, ssq_sem_in,
):
    s, t = lax.axis_index("seq"), lax.axis_index("tp")
    y, g = s % 2, s // 2
    rows, feats = tokens_ref.shape
    mate = t + 1 - 2 * (t % 2)
    across = (t + 2) % 4
    diagonal = (mate + 2) % 4
    partner = s + 1 - 2 * y
    last = pairs - 1

    def remote(src, dst, send, recv, where):
        return pltpu.make_async_remote_copy(
            src_ref=src, dst_ref=dst, send_sem=send, recv_sem=recv,
            device_id=where, device_id_type=MESH)

    own_tokens = pltpu.make_async_copy(tokens_ref, tok.at[t], tok_sem)
    own_tokens.start()
    loads = [
        pltpu.make_async_copy(src, dst, load_sem.at[i])
        for i, (src, dst) in enumerate([(wk_hbm, wk), (wv_hbm, wv), (wq_hbm, wq), (wg_hbm, wg)])
    ]
    loads += [
        pltpu.make_async_copy(wo_hbm.at[:, pl.ds(j * feats, feats)], wo.at[j], load_sem.at[4 + j])
        for j in range(4)
    ]
    for load in loads:
        load.start()

    barrier = pltpu.get_barrier_semaphore()
    up_g, down_g = (g + 1) % pairs, (g + last) % pairs
    skew = ((g + y * 2 - 1 + pairs) % pairs) * 2 + 1 - y
    for device in ((s, mate), (s, across), (s, diagonal), (partner, t), (up_g * 2 + y, t), (down_g * 2 + y, t), (skew, t)):
        pl.semaphore_signal(barrier, inc=1, device_id=device, device_id_type=MESH)
    id_row = ids_ref[...].astype(F32)
    id_last = id_row[:, rows - 1:rows]
    id_out[...] = jnp.broadcast_to(id_last, id_out.shape)
    acc_q[...] = jnp.zeros_like(acc_q)
    acc_k[...] = jnp.zeros_like(acc_k)
    acc_v[...] = jnp.zeros_like(acc_v)
    acc_g[...] = jnp.zeros_like(acc_g)
    acc_low[...] = jnp.zeros_like(acc_low)
    own_tokens.wait()
    own = tok[t].astype(F32)
    squares = jnp.sum(own * own, axis=-1, keepdims=True)
    ssq_all[0] = jnp.broadcast_to(squares, (rows, 128)).T[0:8]
    pl.semaphore_wait(barrier, 7)
    send_ssq = [
        remote(ssq_all.at[0], ssq_all.at[i + 1], ssq_sem.at[i], ssq_sem_in.at[i], (s, peer))
        for i, peer in enumerate((mate, across, diagonal))
    ]
    for copy in send_ssq:
        copy.start()

    size = rows // TOKEN_CHUNKS

    def piece(block, c):
        return tok.at[block, pl.ds(c * size, size)]

    to_x = [remote(piece(t, c), piece(t, c), tok_x.at[c], tok_x_in.at[c], (s, across)) for c in range(TOKEN_CHUNKS)]
    to_mate = [remote(piece(t, c), piece(t, c), tok_mate.at[c], tok_mate_in.at[c], (s, mate)) for c in range(TOKEN_CHUNKS)]
    from_x = [remote(piece(across, c), piece(across, c), tok_x.at[c], tok_x_in.at[c], (s, across)) for c in range(TOKEN_CHUNKS)]
    from_mate = [remote(piece(mate, c), piece(mate, c), tok_mate.at[c], tok_mate_in.at[c], (s, mate)) for c in range(TOKEN_CHUNKS)]
    forward = [remote(piece(across, c), piece(across, c), tok_fwd.at[c], tok_fwd_in.at[c], (s, mate)) for c in range(TOKEN_CHUNKS)]
    from_fwd = [remote(piece(diagonal, c), piece(diagonal, c), tok_fwd.at[c], tok_fwd_in.at[c], (s, mate)) for c in range(TOKEN_CHUNKS)]
    for c in range(TOKEN_CHUNKS):
        to_x[c].start()
        to_mate[c].start()

    send_id = remote(id_out, id_in, id_sem.at[0], id_sem.at[1], (s + 1, t))

    @pl.when(s < 2 * pairs - 1)
    def _():
        send_id.start()

    def normed(block):
        return (tok[block].astype(F32) * r * gain_ref[block]).astype(BF16)

    def project_state(block):
        xg = normed(block)
        acc_low[...] += dot_nt(xg, down_ref[:, pl.ds(pl.multiple_of(block * feats, feats), feats)])
        acc_k[...] += dot(xg, wk[block])
        acc_v[...] += dot(xg, wv[block])

    def project_read(block):
        xg = normed(block)
        acc_q[...] += dot(xg, wq[block])
        acc_g[...] += dot(xg, wg[block])

    for copy in send_ssq:
        copy.wait_recv()
    total = ssq_all[0] + ssq_all[1] + ssq_all[2] + ssq_all[3]
    scale_row = lax.rsqrt(total / (4 * feats) + 1e-5)[0:1]
    r = jnp.broadcast_to(scale_row, (128, rows)).T[:, 0:1]
    for load in loads[:4]:
        load.wait()
    project_state(t)
    project_read(t)
    from_x[0].wait_recv()
    forward[0].start()
    for c in range(TOKEN_CHUNKS):
        from_mate[c].wait_recv()
    project_state(mate)
    project_read(mate)
    for c in range(1, TOKEN_CHUNKS):
        from_x[c].wait_recv()
        forward[c].start()
    project_state(across)
    project_read(across)
    for c in range(TOKEN_CHUNKS):
        from_fwd[c].wait_recv()
    project_state(diagonal)

    low = acc_low[...].astype(BF16)
    z = dot(low, up_ref[...]) + bias_ref[...]
    rate = (jnp.minimum(z, 0.0) - jnp.log1p(jnp.exp(-jnp.abs(z)))) / 16.0
    row = lax.broadcasted_iota(jnp.int32, (rows, rows), 0)
    col = lax.broadcasted_iota(jnp.int32, (rows, rows), 1)
    within = jnp.where((row // C == col // C) & (col <= row), 1.0, 0.0).astype(BF16)
    high = rate.astype(BF16)
    rest = rate - high.astype(F32)
    middle = rest.astype(BF16)
    tiny = (rest - middle.astype(F32)).astype(BF16)
    cum = dot(within, high) + dot(within, middle) + dot(within, tiny)
    blocks = rows // C
    totals = [cum[(b + 1) * C - 1:(b + 1) * C] for b in range(blocks)]
    id_col = jnp.broadcast_to(id_row, (rows, rows)).T

    @pl.when(s == 0)
    def _():
        id_in[...] = jnp.full_like(id_in, -1.0)

    @pl.when(s > 0)
    def _():
        send_id.wait_recv()

    id_prev = id_in[0:1, 0:1]
    key = acc_k[...].astype(BF16).astype(F32)
    value = acc_v[...].astype(BF16)
    keep = jnp.where(id_col[:, 0:1] == id_last, 1.0, 0.0)
    zero = jnp.zeros_like(totals[0])
    kend, kdev = [], []
    for b in range(blocks):
        mine = slice(b * C, (b + 1) * C)
        end = key[mine] * jnp.exp(totals[b] - cum[mine])
        kend.append(end)
        kdev.append((end * jnp.exp(sum(totals[b + 1:], zero)) * keep[mine]).astype(BF16))
    state = dot_tn(value, jnp.concatenate(kdev, axis=0))
    s_own[...] = state.astype(BF16)
    going_on = jnp.where(id_last == id_prev, 1.0, 0.0)
    p_own[...] = jnp.broadcast_to(jnp.exp(sum(totals, zero)) * going_on, p_own.shape)

    half = V // 2
    span = half // STATE_CHUNKS

    def part(ref, owner, c):
        return ref.at[pl.ds(pl.multiple_of(owner * half + c * span, span), span)]

    def small(ref, c):
        return ref.at[pl.ds(c * span, span)]

    send_p = remote(p_own, p_other, p_sem.at[0], p_sem.at[1], (partner, t))
    send_p.start()
    swap = [remote(part(s_own, 1 - y, c), small(s_other, c), s_sem.at[c], s_sem_in.at[c], (partner, t)) for c in range(STATE_CHUNKS)]
    for c in range(STATE_CHUNKS):
        swap[c].start()
    chain = [remote(small(e_out, c), small(e_in, c), e_sem.at[c], e_sem_in.at[c], (s + 2, t)) for c in range(STATE_CHUNKS)]
    give = [remote(small(i_out, c), part(incoming, y, c), i_sem.at[c], i_sem_in.at[c], (partner, t)) for c in range(STATE_CHUNKS)]
    take = [remote(small(i_out, c), part(incoming, 1 - y, c), i_sem.at[c], i_sem_in.at[c], (partner, t)) for c in range(STATE_CHUNKS)]

    project_read(diagonal)
    grow = jnp.exp(cum)
    query = acc_q[...].astype(BF16).astype(F32)
    qdec = (query * grow * K ** -0.5).astype(BF16)
    kinv = (key * jnp.exp(-cum)).astype(BF16)
    from_prev = jnp.where(id_col[:, 0:1] == id_prev, 1.0, 0.0)
    for b in range(blocks):
        mine = slice(b * C, (b + 1) * C)
        seen = (b + 1) * C
        keys = [
            (kend[a] * jnp.exp(sum(totals[a + 1:b], zero))).astype(BF16) for a in range(b)
        ] + [kinv[mine]]
        scores = dot_nt(qdec[mine], jnp.concatenate(keys, axis=0))
        allowed = (col[mine, :seen] <= row[mine, :seen]) & (id_col[mine, :seen] == id_row[:, :seen])
        weights = jnp.where(allowed, scores, 0.0).astype(BF16)
        attn_ref[mine, :] = dot(weights, value[:seen])
        qin_ref[mine, :] = (
            qdec[mine].astype(F32) * jnp.exp(sum(totals[:b], zero)) * from_prev[mine]
        ).astype(BF16)

    @pl.when(g == 0)
    def _():
        e_in[...] = jnp.zeros_like(e_in)

    second = y.astype(F32)
    first = 1.0 - second
    send_p.wait_recv()
    own_decay, other_decay = p_own[0:1, :], p_other[0:1, :]
    p0 = own_decay * first + other_decay * second
    p1 = own_decay * second + other_decay * first
    both = p0 * p1

    def place(c):
        return pl.ds(pl.multiple_of(y * half + c * span, span), span)

    for c in range(STATE_CHUNKS):
        swap[c].wait_recv()
        mine = pl.ds(c * span, span)
        a, b = s_own[place(c), :].astype(F32), s_other[mine, :].astype(F32)
        s0 = a * first + b * second
        s1 = a * second + b * first
        pair_first[mine, :] = s0
        pair_state[mine, :] = p1 * s0 + s1

    for c in range(STATE_CHUNKS):
        mine = pl.ds(c * span, span)

        @pl.when(g > 0)
        def _():
            chain[c].wait_recv()

        @pl.when(g < last)
        def _():
            e_out[mine, :] = (both * e_in[mine, :].astype(F32) + pair_state[mine, :]).astype(BF16)
            chain[c].start()

        entry = e_in[mine, :].astype(F32)
        middle_state = p0 * entry + pair_first[mine, :]
        i_out[mine, :] = (middle_state * first + entry * second).astype(BF16)
        give[c].start()
        incoming[place(c), :] = (entry * first + middle_state * second).astype(BF16)
    opengate = acc_g[...]
    acc_g[...] = head_gain_ref[...] * (opengate * jax.nn.sigmoid(opengate))
    for load in loads[4:]:
        load.wait()
    for c in range(STATE_CHUNKS):
        take[c].wait_recv()

    lot = rows // OUT_CHUNKS

    def lines(c):
        return pl.ds(c * lot, lot)

    share = [
        [remote(mate_out.at[k, lines(c)], mate_in.at[k, lines(c)], m_sem.at[k, c], m_sem_in.at[k, c], (s, mate)) for c in range(OUT_CHUNKS)]
        for k in range(2)
    ]
    over = [remote(x_out.at[lines(c)], x_in.at[lines(c)], x_sem.at[c], x_sem_in.at[c], (s, across)) for c in range(OUT_CHUNKS)]
    for c in range(OUT_CHUNKS):
        attn = attn_ref[lines(c), :] + dot_nt(qin_ref[lines(c), :], incoming[...])
        scale = lax.rsqrt(jnp.mean(attn * attn, axis=-1, keepdims=True) + 1e-5)
        gated_ref[lines(c), :] = (attn * scale * acc_g[lines(c), :]).astype(BF16)
        mate_out[0, lines(c), :] = dot(gated_ref[lines(c), :], wo[diagonal]).astype(BF16)
        share[0][c].start()
        keep_x[lines(c), :] = dot(gated_ref[lines(c), :], wo[across])
    for c in range(OUT_CHUNKS):
        share[0][c].wait_recv()
        x_out[lines(c), :] = (keep_x[lines(c), :] + mate_in[0, lines(c), :].astype(F32)).astype(BF16)
        over[c].start()
    for c in range(OUT_CHUNKS):
        mate_out[1, lines(c), :] = dot(gated_ref[lines(c), :], wo[mate]).astype(BF16)
        share[1][c].start()
        keep_own[lines(c), :] = dot(gated_ref[lines(c), :], wo[t])
    for c in range(OUT_CHUNKS):
        share[1][c].wait_recv()
        over[c].wait_recv()
        out_ref[lines(c), :] = (
            keep_own[lines(c), :] + mate_in[1, lines(c), :].astype(F32) + x_in[lines(c), :].astype(F32)
        ).astype(BF16)

    for copy in to_x + to_mate + forward + send_ssq + [send_p] + swap + give + share[0] + share[1] + over:
        copy.wait_send()

    @pl.when(s < 2 * pairs - 1)
    def _():
        send_id.wait_send()

    @pl.when(g < last)
    def _():
        for c in range(STATE_CHUNKS):
            chain[c].wait_send()


def per_device(
    pairs,
    tokens, norm_gain, w_query, w_key, w_value, w_gate_out, gate_down, gate_up, gate_bias,
    head_gain, w_out, request_ids,
):
    rows, feats = tokens.shape
    ranks = gate_down.shape[1]
    vmem = pl.BlockSpec(memory_space=pltpu.VMEM)
    hbm = pl.BlockSpec(memory_space=pl.ANY)
    half = V // 2
    dma = pltpu.SemaphoreType.DMA
    scratch = [
        pltpu.VMEM((4, rows, feats), BF16),
        pltpu.VMEM((4, feats, K), BF16),
        pltpu.VMEM((4, feats, K), BF16),
        pltpu.VMEM((4, feats, V), BF16),
        pltpu.VMEM((4, feats, V), BF16),
        pltpu.VMEM((4, V, feats), BF16),
        pltpu.VMEM((rows, K), F32),
        pltpu.VMEM((rows, K), F32),
        pltpu.VMEM((rows, V), F32),
        pltpu.VMEM((rows, V), F32),
        pltpu.VMEM((rows, ranks), F32),
        pltpu.VMEM((4, 8, rows), F32),
        pltpu.VMEM((rows, V), F32),
        pltpu.VMEM((rows, K), BF16),
        pltpu.VMEM((rows, V), BF16),
        pltpu.VMEM((8, 128), F32),
        pltpu.VMEM((8, 128), F32),
        pltpu.VMEM((8, K), F32),
        pltpu.VMEM((8, K), F32),
        pltpu.VMEM((V, K), BF16),
        pltpu.VMEM((half, K), BF16),
        pltpu.VMEM((half, K), BF16),
        pltpu.VMEM((half, K), BF16),
        pltpu.VMEM((half, K), BF16),
        pltpu.VMEM((V, K), BF16),
        pltpu.VMEM((2, rows, feats), BF16),
        pltpu.VMEM((2, rows, feats), BF16),
        pltpu.VMEM((rows, feats), BF16),
        pltpu.VMEM((rows, feats), BF16),
        pltpu.VMEM((rows, feats), F32),
        pltpu.VMEM((rows, feats), F32),
        pltpu.VMEM((half, K), F32),
        pltpu.VMEM((half, K), F32),
        dma((8,)),
        dma,
        dma((TOKEN_CHUNKS,)), dma((TOKEN_CHUNKS,)),
        dma((TOKEN_CHUNKS,)), dma((TOKEN_CHUNKS,)),
        dma((TOKEN_CHUNKS,)), dma((TOKEN_CHUNKS,)),
        dma((2,)), dma((2,)),
        dma((STATE_CHUNKS,)), dma((STATE_CHUNKS,)),
        dma((STATE_CHUNKS,)), dma((STATE_CHUNKS,)),
        dma((STATE_CHUNKS,)), dma((STATE_CHUNKS,)),
        dma((2, OUT_CHUNKS)), dma((2, OUT_CHUNKS)),
        dma((OUT_CHUNKS,)), dma((OUT_CHUNKS,)),
        dma((3,)), dma((3,)),
    ]
    return pl.pallas_call(
        functools.partial(kernel, pairs),
        out_shape=jax.ShapeDtypeStruct((rows, feats), BF16),
        in_specs=[hbm, vmem, hbm, hbm, hbm, hbm, vmem, vmem, vmem, vmem, hbm, vmem],
        out_specs=vmem,
        scratch_shapes=scratch,
        compiler_params=pltpu.CompilerParams(
            collective_id=0, has_side_effects=True, vmem_limit_bytes=62 * 2**20),
        cost_estimate=pl.CostEstimate(flops=2_500_000_000, bytes_accessed=10_000_000, transcendentals=400_000),
        name="gla",
    )(
        tokens,
        norm_gain.reshape(4, 1, feats),
        w_query.reshape(4, feats, K),
        w_key.reshape(4, feats, K),
        w_value.reshape(4, feats, V),
        w_gate_out.reshape(4, feats, V),
        gate_down.T,
        gate_up,
        gate_bias.reshape(1, K),
        head_gain.reshape(1, V),
        w_out,
        request_ids.reshape(1, rows),
    )


def solution(mesh):
    return jax.shard_map(
        functools.partial(per_device, mesh.shape["seq"] // 2),
        mesh=mesh,
        in_specs=(
            P("seq", "tp"),
            P(),
            P(None, "tp"),
            P(None, "tp"),
            P(None, "tp"),
            P(None, "tp"),
            P(),
            P(None, "tp"),
            P("tp"),
            P("tp"),
            P("tp", None),
            P("seq"),
        ),
        out_specs=P("seq", "tp"),
        check_vma=False,
    )
```

```python
import functools

import jax
import jax.numpy as jnp
from jax import lax
from jax.experimental import pallas as pl
from jax.experimental.pallas import tpu as pltpu
from jax.sharding import PartitionSpec as P

K = 256
V = 512
C = 64
F32 = jnp.float32
BF16 = jnp.bfloat16
MESH = pl.DeviceIdType.MESH
TOKEN_CHUNKS = 4
STATE_CHUNKS = 4
OUT_CHUNKS = 2


def dot(a, b):
    return jnp.dot(a, b, preferred_element_type=F32)


def dot_nt(a, b):
    return lax.dot_general(a, b, (((1,), (1,)), ((), ())), preferred_element_type=F32)


def dot_tn(a, b):
    return lax.dot_general(a, b, (((0,), (0,)), ((), ())), preferred_element_type=F32)


def kernel(
    pairs,
    tokens_ref, gain_ref, wq_hbm, wk_hbm, wv_hbm, wg_hbm, down_ref, up_ref, bias_ref,
    head_gain_ref, wo_hbm, ids_ref,
    out_ref,
    tok, wq, wk, wv, wg, wo,
    acc_q, acc_k, acc_v, acc_g, acc_low, ssq_all,
    attn_ref, qin_ref, gated_ref,
    id_out, id_in, p_own, p_other,
    s_own, s_other, e_in, e_out, i_out, incoming,
    mate_out, mate_in, x_out, x_in, keep_x, keep_own, pair_first,
    load_sem, tok_sem, tok_x, tok_x_in, tok_mate, tok_mate_in, tok_fwd, tok_fwd_in,
    id_sem, p_sem, s_sem, s_sem_in, e_sem, e_sem_in, i_sem, i_sem_in,
    m_sem, m_sem_in, x_sem, x_sem_in, ssq_sem, ssq_sem_in,
):
    s, t = lax.axis_index("seq"), lax.axis_index("tp")
    y, g = s % 2, s // 2
    rows, feats = tokens_ref.shape
    mate = t + 1 - 2 * (t % 2)
    across = (t + 2) % 4
    diagonal = (mate + 2) % 4
    partner = s + 1 - 2 * y
    last = pairs - 1

    def remote(src, dst, send, recv, where):
        return pltpu.make_async_remote_copy(
            src_ref=src, dst_ref=dst, send_sem=send, recv_sem=recv,
            device_id=where, device_id_type=MESH)

    own_tokens = pltpu.make_async_copy(tokens_ref, tok.at[t], tok_sem)
    own_tokens.start()
    loads = [
        pltpu.make_async_copy(src, dst, load_sem.at[i])
        for i, (src, dst) in enumerate([(wk_hbm, wk), (wv_hbm, wv), (wq_hbm, wq), (wg_hbm, wg)])
    ]
    loads += [
        pltpu.make_async_copy(wo_hbm.at[:, pl.ds(j * feats, feats)], wo.at[j], load_sem.at[4 + j])
        for j in range(4)
    ]
    for load in loads:
        load.start()

    barrier = pltpu.get_barrier_semaphore()
    up_g, down_g = (g + 1) % pairs, (g + last) % pairs
    skew = ((g + y * 2 - 1 + pairs) % pairs) * 2 + 1 - y
    for device in ((s, mate), (s, across), (s, diagonal), (partner, t), (up_g * 2 + y, t), (down_g * 2 + y, t), (skew, t)):
        pl.semaphore_signal(barrier, inc=1, device_id=device, device_id_type=MESH)
    id_row = ids_ref[...].astype(F32)
    id_last = id_row[:, rows - 1:rows]
    id_out[...] = jnp.broadcast_to(id_last, id_out.shape)
    acc_q[...] = jnp.zeros_like(acc_q)
    acc_k[...] = jnp.zeros_like(acc_k)
    acc_v[...] = jnp.zeros_like(acc_v)
    acc_g[...] = jnp.zeros_like(acc_g)
    acc_low[...] = jnp.zeros_like(acc_low)
    own_tokens.wait()
    own = tok[t].astype(F32)
    squares = jnp.sum(own * own, axis=-1, keepdims=True)
    ssq_all[0] = jnp.broadcast_to(squares, (rows, 128)).T[0:8]
    pl.semaphore_wait(barrier, 7)
    send_ssq = [
        remote(ssq_all.at[0], ssq_all.at[i + 1], ssq_sem.at[i], ssq_sem_in.at[i], (s, peer))
        for i, peer in enumerate((mate, across, diagonal))
    ]
    for copy in send_ssq:
        copy.start()

    size = rows // TOKEN_CHUNKS

    def piece(block, c):
        return tok.at[block, pl.ds(c * size, size)]

    to_x = [remote(piece(t, c), piece(t, c), tok_x.at[c], tok_x_in.at[c], (s, across)) for c in range(TOKEN_CHUNKS)]
    to_mate = [remote(piece(t, c), piece(t, c), tok_mate.at[c], tok_mate_in.at[c], (s, mate)) for c in range(TOKEN_CHUNKS)]
    from_x = [remote(piece(across, c), piece(across, c), tok_x.at[c], tok_x_in.at[c], (s, across)) for c in range(TOKEN_CHUNKS)]
    from_mate = [remote(piece(mate, c), piece(mate, c), tok_mate.at[c], tok_mate_in.at[c], (s, mate)) for c in range(TOKEN_CHUNKS)]
    forward = [remote(piece(across, c), piece(across, c), tok_fwd.at[c], tok_fwd_in.at[c], (s, mate)) for c in range(TOKEN_CHUNKS)]
    from_fwd = [remote(piece(diagonal, c), piece(diagonal, c), tok_fwd.at[c], tok_fwd_in.at[c], (s, mate)) for c in range(TOKEN_CHUNKS)]
    for c in range(TOKEN_CHUNKS):
        to_x[c].start()
        to_mate[c].start()

    send_id = remote(id_out, id_in, id_sem.at[0], id_sem.at[1], (s + 1, t))

    @pl.when(s < 2 * pairs - 1)
    def _():
        send_id.start()

    def normed(block):
        return (tok[block].astype(F32) * r * gain_ref[block]).astype(BF16)

    def project_state(block):
        xg = normed(block)
        acc_low[...] += dot_nt(xg, down_ref[:, pl.ds(pl.multiple_of(block * feats, feats), feats)])
        acc_k[...] += dot(xg, wk[block])
        acc_v[...] += dot(xg, wv[block])

    def project_read(block):
        xg = normed(block)
        acc_q[...] += dot(xg, wq[block])
        acc_g[...] += dot(xg, wg[block])

    for copy in send_ssq:
        copy.wait_recv()
    total = ssq_all[0] + ssq_all[1] + ssq_all[2] + ssq_all[3]
    scale_row = lax.rsqrt(total / (4 * feats) + 1e-5)[0:1]
    r = jnp.broadcast_to(scale_row, (128, rows)).T[:, 0:1]
    for load in loads[:4]:
        load.wait()
    project_state(t)
    project_read(t)
    from_x[0].wait_recv()
    forward[0].start()
    for c in range(TOKEN_CHUNKS):
        from_mate[c].wait_recv()
    project_state(mate)
    project_read(mate)
    for c in range(1, TOKEN_CHUNKS):
        from_x[c].wait_recv()
        forward[c].start()
    project_state(across)
    project_read(across)
    for c in range(TOKEN_CHUNKS):
        from_fwd[c].wait_recv()
    project_state(diagonal)

    low = acc_low[...].astype(BF16)
    z = dot(low, up_ref[...]) + bias_ref[...]
    rate = (jnp.minimum(z, 0.0) - jnp.log1p(jnp.exp(-jnp.abs(z)))) / 16.0
    row = lax.broadcasted_iota(jnp.int32, (rows, rows), 0)
    col = lax.broadcasted_iota(jnp.int32, (rows, rows), 1)
    within = jnp.where((row // C == col // C) & (col <= row), 1.0, 0.0).astype(BF16)
    high = rate.astype(BF16)
    rest = rate - high.astype(F32)
    middle = rest.astype(BF16)
    tiny = (rest - middle.astype(F32)).astype(BF16)
    cum = dot(within, high) + dot(within, middle) + dot(within, tiny)
    blocks = rows // C
    totals = [cum[(b + 1) * C - 1:(b + 1) * C] for b in range(blocks)]
    id_col = jnp.broadcast_to(id_row, (rows, rows)).T

    @pl.when(s == 0)
    def _():
        id_in[...] = jnp.full_like(id_in, -1.0)

    @pl.when(s > 0)
    def _():
        send_id.wait_recv()

    id_prev = id_in[0:1, 0:1]
    key = acc_k[...].astype(BF16).astype(F32)
    value = acc_v[...].astype(BF16)
    keep = jnp.where(id_col[:, 0:1] == id_last, 1.0, 0.0)
    zero = jnp.zeros_like(totals[0])
    kend, kdev = [], []
    for b in range(blocks):
        mine = slice(b * C, (b + 1) * C)
        end = key[mine] * jnp.exp(totals[b] - cum[mine])
        kend.append(end)
        kdev.append((end * jnp.exp(sum(totals[b + 1:], zero)) * keep[mine]).astype(BF16))
    state = dot_tn(value, jnp.concatenate(kdev, axis=0))
    s_own[...] = state.astype(BF16)
    going_on = jnp.where(id_last == id_prev, 1.0, 0.0)
    p_own[...] = jnp.broadcast_to(jnp.exp(sum(totals, zero)) * going_on, p_own.shape)

    half = V // 2
    span = half // STATE_CHUNKS

    def part(ref, owner, c):
        return ref.at[pl.ds(pl.multiple_of(owner * half + c * span, span), span)]

    def small(ref, c):
        return ref.at[pl.ds(c * span, span)]

    send_p = remote(p_own, p_other, p_sem.at[0], p_sem.at[1], (partner, t))
    send_p.start()
    swap = [remote(part(s_own, 1 - y, c), small(s_other, c), s_sem.at[c], s_sem_in.at[c], (partner, t)) for c in range(STATE_CHUNKS)]
    for c in range(STATE_CHUNKS):
        swap[c].start()
    reach = pairs // 2
    chain = [
        [remote(small(e_out.at[k], c), small(e_in.at[k], c), e_sem.at[k, c], e_sem_in.at[k, c], (s + 2, t)) for c in range(STATE_CHUNKS)]
        for k in range(reach)
    ]
    give = [remote(small(i_out, c), part(incoming, y, c), i_sem.at[c], i_sem_in.at[c], (partner, t)) for c in range(STATE_CHUNKS)]
    take = [remote(small(i_out, c), part(incoming, 1 - y, c), i_sem.at[c], i_sem_in.at[c], (partner, t)) for c in range(STATE_CHUNKS)]

    project_read(diagonal)
    grow = jnp.exp(cum)
    query = acc_q[...].astype(BF16).astype(F32)
    qdec = (query * grow * K ** -0.5).astype(BF16)
    kinv = (key * jnp.exp(-cum)).astype(BF16)
    from_prev = jnp.where(id_col[:, 0:1] == id_prev, 1.0, 0.0)
    for b in range(blocks):
        mine = slice(b * C, (b + 1) * C)
        seen = (b + 1) * C
        keys = [
            (kend[a] * jnp.exp(sum(totals[a + 1:b], zero))).astype(BF16) for a in range(b)
        ] + [kinv[mine]]
        scores = dot_nt(qdec[mine], jnp.concatenate(keys, axis=0))
        allowed = (col[mine, :seen] <= row[mine, :seen]) & (id_col[mine, :seen] == id_row[:, :seen])
        weights = jnp.where(allowed, scores, 0.0).astype(BF16)
        attn_ref[mine, :] = dot(weights, value[:seen])
        qin_ref[mine, :] = (
            qdec[mine].astype(F32) * jnp.exp(sum(totals[:b], zero)) * from_prev[mine]
        ).astype(BF16)

    for k in range(reach):
        @pl.when(g <= k)
        def _():
            e_in[k] = jnp.zeros_like(e_in[k])

    second = y.astype(F32)
    first = 1.0 - second
    send_p.wait_recv()
    own_decay, other_decay = p_own[0:1, :], p_other[0:1, :]
    p0 = own_decay * first + other_decay * second
    p1 = own_decay * second + other_decay * first
    both = p0 * p1

    def place(c):
        return pl.ds(pl.multiple_of(y * half + c * span, span), span)

    for c in range(STATE_CHUNKS):
        swap[c].wait_recv()
        mine = pl.ds(c * span, span)
        a, b = s_own[place(c), :].astype(F32), s_other[mine, :].astype(F32)
        s0 = a * first + b * second
        s1 = a * second + b * first
        pair_first[mine, :] = s0

        @pl.when(g < last)
        def _():
            e_out[0, mine, :] = (p1 * s0 + s1).astype(BF16)
            chain[0][c].start()

    for k in range(1, reach):
        for c in range(STATE_CHUNKS):
            mine = pl.ds(c * span, span)

            @pl.when(g >= k)
            def _():
                chain[k - 1][c].wait_recv()

            @pl.when((g >= k) & (g < last))
            def _():
                e_out[k, mine, :] = (both * e_in[k - 1, mine, :].astype(F32)).astype(BF16)
                chain[k][c].start()

    for c in range(STATE_CHUNKS):
        mine = pl.ds(c * span, span)

        @pl.when(g >= reach)
        def _():
            chain[reach - 1][c].wait_recv()

        entry = e_in[0, mine, :].astype(F32)
        for k in range(1, reach):
            entry += e_in[k, mine, :].astype(F32)
        middle_state = p0 * entry + pair_first[mine, :]
        i_out[mine, :] = (middle_state * first + entry * second).astype(BF16)
        give[c].start()
        incoming[place(c), :] = (entry * first + middle_state * second).astype(BF16)
    opengate = acc_g[...]
    acc_g[...] = head_gain_ref[...] * (opengate * jax.nn.sigmoid(opengate))
    for load in loads[4:]:
        load.wait()
    for c in range(STATE_CHUNKS):
        take[c].wait_recv()

    lot = rows // OUT_CHUNKS

    def lines(c):
        return pl.ds(c * lot, lot)

    share = [
        [remote(mate_out.at[k, lines(c)], mate_in.at[k, lines(c)], m_sem.at[k, c], m_sem_in.at[k, c], (s, mate)) for c in range(OUT_CHUNKS)]
        for k in range(2)
    ]
    over = [remote(x_out.at[lines(c)], x_in.at[lines(c)], x_sem.at[c], x_sem_in.at[c], (s, across)) for c in range(OUT_CHUNKS)]
    attn_ref[...] += dot_nt(qin_ref[...], incoming[...])
    for c in range(OUT_CHUNKS):
        attn = attn_ref[lines(c), :]
        scale = lax.rsqrt(jnp.mean(attn * attn, axis=-1, keepdims=True) + 1e-5)
        gated_ref[lines(c), :] = (attn * scale * acc_g[lines(c), :]).astype(BF16)
        mate_out[0, lines(c), :] = dot(gated_ref[lines(c), :], wo[diagonal]).astype(BF16)
        share[0][c].start()
        keep_x[lines(c), :] = dot(gated_ref[lines(c), :], wo[across])
    for c in range(OUT_CHUNKS):
        share[0][c].wait_recv()
        x_out[lines(c), :] = (keep_x[lines(c), :] + mate_in[0, lines(c), :].astype(F32)).astype(BF16)
        over[c].start()
    for c in range(OUT_CHUNKS):
        mate_out[1, lines(c), :] = dot(gated_ref[lines(c), :], wo[mate]).astype(BF16)
        share[1][c].start()
        keep_own[lines(c), :] = dot(gated_ref[lines(c), :], wo[t])
    for c in range(OUT_CHUNKS):
        share[1][c].wait_recv()
        over[c].wait_recv()
        out_ref[lines(c), :] = (
            keep_own[lines(c), :] + mate_in[1, lines(c), :].astype(F32) + x_in[lines(c), :].astype(F32)
        ).astype(BF16)

    for copy in to_x + to_mate + forward + send_ssq + [send_p] + swap + give + share[0] + share[1] + over:
        copy.wait_send()

    @pl.when(s < 2 * pairs - 1)
    def _():
        send_id.wait_send()

    for k in range(reach):
        @pl.when((g >= k) & (g < last))
        def _():
            for c in range(STATE_CHUNKS):
                chain[k][c].wait_send()


def per_device(
    pairs,
    tokens, norm_gain, w_query, w_key, w_value, w_gate_out, gate_down, gate_up, gate_bias,
    head_gain, w_out, request_ids,
):
    rows, feats = tokens.shape
    ranks = gate_down.shape[1]
    vmem = pl.BlockSpec(memory_space=pltpu.VMEM)
    hbm = pl.BlockSpec(memory_space=pl.ANY)
    half = V // 2
    dma = pltpu.SemaphoreType.DMA
    scratch = [
        pltpu.VMEM((4, rows, feats), BF16),
        pltpu.VMEM((4, feats, K), BF16),
        pltpu.VMEM((4, feats, K), BF16),
        pltpu.VMEM((4, feats, V), BF16),
        pltpu.VMEM((4, feats, V), BF16),
        pltpu.VMEM((4, V, feats), BF16),
        pltpu.VMEM((rows, K), F32),
        pltpu.VMEM((rows, K), F32),
        pltpu.VMEM((rows, V), F32),
        pltpu.VMEM((rows, V), F32),
        pltpu.VMEM((rows, ranks), F32),
        pltpu.VMEM((4, 8, rows), F32),
        pltpu.VMEM((rows, V), F32),
        pltpu.VMEM((rows, K), BF16),
        pltpu.VMEM((rows, V), BF16),
        pltpu.VMEM((8, 128), F32),
        pltpu.VMEM((8, 128), F32),
        pltpu.VMEM((8, K), F32),
        pltpu.VMEM((8, K), F32),
        pltpu.VMEM((V, K), BF16),
        pltpu.VMEM((half, K), BF16),
        pltpu.VMEM((pairs // 2, half, K), BF16),
        pltpu.VMEM((pairs // 2, half, K), BF16),
        pltpu.VMEM((half, K), BF16),
        pltpu.VMEM((V, K), BF16),
        pltpu.VMEM((2, rows, feats), BF16),
        pltpu.VMEM((2, rows, feats), BF16),
        pltpu.VMEM((rows, feats), BF16),
        pltpu.VMEM((rows, feats), BF16),
        pltpu.VMEM((rows, feats), F32),
        pltpu.VMEM((rows, feats), F32),
        pltpu.VMEM((half, K), F32),
        dma((8,)),
        dma,
        dma((TOKEN_CHUNKS,)), dma((TOKEN_CHUNKS,)),
        dma((TOKEN_CHUNKS,)), dma((TOKEN_CHUNKS,)),
        dma((TOKEN_CHUNKS,)), dma((TOKEN_CHUNKS,)),
        dma((2,)), dma((2,)),
        dma((STATE_CHUNKS,)), dma((STATE_CHUNKS,)),
        dma((pairs // 2, STATE_CHUNKS)), dma((pairs // 2, STATE_CHUNKS)),
        dma((STATE_CHUNKS,)), dma((STATE_CHUNKS,)),
        dma((2, OUT_CHUNKS)), dma((2, OUT_CHUNKS)),
        dma((OUT_CHUNKS,)), dma((OUT_CHUNKS,)),
        dma((3,)), dma((3,)),
    ]
    return pl.pallas_call(
        functools.partial(kernel, pairs),
        out_shape=jax.ShapeDtypeStruct((rows, feats), BF16),
        in_specs=[hbm, vmem, hbm, hbm, hbm, hbm, vmem, vmem, vmem, vmem, hbm, vmem],
        out_specs=vmem,
        scratch_shapes=scratch,
        compiler_params=pltpu.CompilerParams(
            collective_id=0, has_side_effects=True, vmem_limit_bytes=62 * 2**20),
        cost_estimate=pl.CostEstimate(flops=2_500_000_000, bytes_accessed=10_000_000, transcendentals=400_000),
        name="gla",
    )(
        tokens,
        norm_gain.reshape(4, 1, feats),
        w_query.reshape(4, feats, K),
        w_key.reshape(4, feats, K),
        w_value.reshape(4, feats, V),
        w_gate_out.reshape(4, feats, V),
        gate_down.T,
        gate_up,
        gate_bias.reshape(1, K),
        head_gain.reshape(1, V),
        w_out,
        request_ids.reshape(1, rows),
    )


def solution(mesh):
    return jax.shard_map(
        functools.partial(per_device, mesh.shape["seq"] // 2),
        mesh=mesh,
        in_specs=(
            P("seq", "tp"),
            P(),
            P(None, "tp"),
            P(None, "tp"),
            P(None, "tp"),
            P(None, "tp"),
            P(),
            P(None, "tp"),
            P("tp"),
            P("tp"),
            P("tp", None),
            P("seq"),
        ),
        out_specs=P("seq", "tp"),
        check_vma=False,
    )
```

```python
import functools

import jax
import jax.numpy as jnp
from jax import lax
from jax.experimental import pallas as pl
from jax.experimental.pallas import tpu as pltpu
from jax.sharding import PartitionSpec as P

K = 256
V = 512
C = 64
F32 = jnp.float32
BF16 = jnp.bfloat16
MESH = pl.DeviceIdType.MESH
TOKEN_CHUNKS = 4
STATE_CHUNKS = 4
OUT_CHUNKS = 2


def dot(a, b):
    return jnp.dot(a, b, preferred_element_type=F32)


def dot_nt(a, b):
    return lax.dot_general(a, b, (((1,), (1,)), ((), ())), preferred_element_type=F32)


def dot_tn(a, b):
    return lax.dot_general(a, b, (((0,), (0,)), ((), ())), preferred_element_type=F32)


def kernel(
    pairs,
    tokens_ref, gain_ref, wq_hbm, wk_hbm, wv_hbm, wg_hbm, down_ref, up_ref, bias_ref,
    head_gain_ref, wo_hbm, ids_ref,
    out_ref,
    tok, wq, wk, wv, wg, wo,
    acc_q, acc_k, acc_v, acc_g, acc_low, ssq_all,
    attn_ref, qin_ref, gated_ref,
    id_out, id_in, p_own, p_other,
    s_own, s_other, e_in, e_out, i_out, incoming,
    mate_out, mate_in, x_out, x_in, keep_own, pair_first,
    load_sem, tok_sem, tok_x, tok_x_in, tok_mate, tok_mate_in, tok_fwd, tok_fwd_in,
    id_sem, p_sem, s_sem, s_sem_in, e_sem, e_sem_in, i_sem, i_sem_in,
    m_sem, m_sem_in, x_sem, x_sem_in, ssq_sem, ssq_sem_in,
):
    s, t = lax.axis_index("seq"), lax.axis_index("tp")
    y, g = s % 2, s // 2
    rows, feats = tokens_ref.shape
    mate = t + 1 - 2 * (t % 2)
    across = (t + 2) % 4
    diagonal = (mate + 2) % 4
    partner = s + 1 - 2 * y
    last = pairs - 1

    def remote(src, dst, send, recv, where):
        return pltpu.make_async_remote_copy(
            src_ref=src, dst_ref=dst, send_sem=send, recv_sem=recv,
            device_id=where, device_id_type=MESH)

    own_tokens = pltpu.make_async_copy(tokens_ref, tok.at[t], tok_sem)
    own_tokens.start()
    loads = [
        pltpu.make_async_copy(src, dst, load_sem.at[i])
        for i, (src, dst) in enumerate([(wk_hbm, wk), (wv_hbm, wv), (wq_hbm, wq), (wg_hbm, wg)])
    ]
    loads += [
        pltpu.make_async_copy(wo_hbm.at[:, pl.ds(j * feats, feats)], wo.at[j], load_sem.at[4 + j])
        for j in range(4)
    ]
    for load in loads:
        load.start()

    barrier = pltpu.get_barrier_semaphore()
    up_g, down_g = (g + 1) % pairs, (g + last) % pairs
    skew = ((g + y * 2 - 1 + pairs) % pairs) * 2 + 1 - y
    for device in ((s, mate), (s, across), (s, diagonal), (partner, t), (up_g * 2 + y, t), (down_g * 2 + y, t), (skew, t)):
        pl.semaphore_signal(barrier, inc=1, device_id=device, device_id_type=MESH)
    id_row = ids_ref[...].astype(F32)
    id_last = id_row[:, rows - 1:rows]
    id_out[...] = jnp.broadcast_to(id_last, id_out.shape)
    acc_q[...] = jnp.zeros_like(acc_q)
    acc_k[...] = jnp.zeros_like(acc_k)
    acc_v[...] = jnp.zeros_like(acc_v)
    acc_g[...] = jnp.zeros_like(acc_g)
    acc_low[...] = jnp.zeros_like(acc_low)
    own_tokens.wait()
    own = tok[t].astype(F32)
    squares = jnp.sum(own * own, axis=-1, keepdims=True)
    ssq_all[0] = jnp.broadcast_to(squares, (rows, 128)).T[0:8]
    pl.semaphore_wait(barrier, 7)
    send_ssq = [
        remote(ssq_all.at[0], ssq_all.at[i + 1], ssq_sem.at[i], ssq_sem_in.at[i], (s, peer))
        for i, peer in enumerate((mate, across, diagonal))
    ]
    for copy in send_ssq:
        copy.start()

    size = rows // TOKEN_CHUNKS

    def piece(block, c):
        return tok.at[block, pl.ds(c * size, size)]

    to_x = [remote(piece(t, c), piece(t, c), tok_x.at[c], tok_x_in.at[c], (s, across)) for c in range(TOKEN_CHUNKS)]
    to_mate = [remote(piece(t, c), piece(t, c), tok_mate.at[c], tok_mate_in.at[c], (s, mate)) for c in range(TOKEN_CHUNKS)]
    from_x = [remote(piece(across, c), piece(across, c), tok_x.at[c], tok_x_in.at[c], (s, across)) for c in range(TOKEN_CHUNKS)]
    from_mate = [remote(piece(mate, c), piece(mate, c), tok_mate.at[c], tok_mate_in.at[c], (s, mate)) for c in range(TOKEN_CHUNKS)]
    forward = [remote(piece(across, c), piece(across, c), tok_fwd.at[c], tok_fwd_in.at[c], (s, mate)) for c in range(TOKEN_CHUNKS)]
    from_fwd = [remote(piece(diagonal, c), piece(diagonal, c), tok_fwd.at[c], tok_fwd_in.at[c], (s, mate)) for c in range(TOKEN_CHUNKS)]
    for c in range(TOKEN_CHUNKS):
        to_x[c].start()
        to_mate[c].start()

    send_id = remote(id_out, id_in, id_sem.at[0], id_sem.at[1], (s + 1, t))

    @pl.when(s < 2 * pairs - 1)
    def _():
        send_id.start()

    def normed(block):
        return (tok[block].astype(F32) * r * gain_ref[block]).astype(BF16)

    def project_state(block):
        xg = normed(block)
        acc_low[...] += dot_nt(xg, down_ref[:, pl.ds(pl.multiple_of(block * feats, feats), feats)])
        acc_k[...] += dot(xg, wk[block])
        acc_v[...] += dot(xg, wv[block])

    def project_read(block):
        xg = normed(block)
        acc_q[...] += dot(xg, wq[block])
        acc_g[...] += dot(xg, wg[block])

    for copy in send_ssq:
        copy.wait_recv()
    total = ssq_all[0] + ssq_all[1] + ssq_all[2] + ssq_all[3]
    scale_row = lax.rsqrt(total / (4 * feats) + 1e-5)[0:1]
    r = jnp.broadcast_to(scale_row, (128, rows)).T[:, 0:1]
    for load in loads[:4]:
        load.wait()
    project_state(t)
    project_read(t)
    from_x[0].wait_recv()
    forward[0].start()
    for c in range(TOKEN_CHUNKS):
        from_mate[c].wait_recv()
    project_state(mate)
    project_read(mate)
    for c in range(1, TOKEN_CHUNKS):
        from_x[c].wait_recv()
        forward[c].start()
    project_state(across)
    project_read(across)
    for c in range(TOKEN_CHUNKS):
        from_fwd[c].wait_recv()
    project_state(diagonal)

    low = acc_low[...].astype(BF16)
    z = dot(low, up_ref[...]) + bias_ref[...]
    rate = (jnp.minimum(z, 0.0) - jnp.log1p(jnp.exp(-jnp.abs(z)))) / 16.0
    row = lax.broadcasted_iota(jnp.int32, (rows, rows), 0)
    col = lax.broadcasted_iota(jnp.int32, (rows, rows), 1)
    within = jnp.where((row // C == col // C) & (col <= row), 1.0, 0.0).astype(BF16)
    high = rate.astype(BF16)
    rest = rate - high.astype(F32)
    middle = rest.astype(BF16)
    tiny = (rest - middle.astype(F32)).astype(BF16)
    cum = dot(within, high) + dot(within, middle) + dot(within, tiny)
    blocks = rows // C
    totals = [cum[(b + 1) * C - 1:(b + 1) * C] for b in range(blocks)]
    id_col = jnp.broadcast_to(id_row, (rows, rows)).T

    @pl.when(s == 0)
    def _():
        id_in[...] = jnp.full_like(id_in, -1.0)

    @pl.when(s > 0)
    def _():
        send_id.wait_recv()

    id_prev = id_in[0:1, 0:1]
    key = acc_k[...].astype(BF16).astype(F32)
    value = acc_v[...].astype(BF16)
    keep = jnp.where(id_col[:, 0:1] == id_last, 1.0, 0.0)
    zero = jnp.zeros_like(totals[0])
    kend, kdev = [], []
    for b in range(blocks):
        mine = slice(b * C, (b + 1) * C)
        end = key[mine] * jnp.exp(totals[b] - cum[mine])
        kend.append(end)
        kdev.append((end * jnp.exp(sum(totals[b + 1:], zero)) * keep[mine]).astype(BF16))
    state = dot_tn(value, jnp.concatenate(kdev, axis=0))
    s_own[...] = state.astype(BF16)
    going_on = jnp.where(id_last == id_prev, 1.0, 0.0)
    p_own[...] = jnp.broadcast_to(jnp.exp(sum(totals, zero)) * going_on, p_own.shape)

    half = V // 2
    span = half // STATE_CHUNKS

    def part(ref, owner, c):
        return ref.at[pl.ds(pl.multiple_of(owner * half + c * span, span), span)]

    def small(ref, c):
        return ref.at[pl.ds(c * span, span)]

    send_p = remote(p_own, p_other, p_sem.at[0], p_sem.at[1], (partner, t))
    send_p.start()
    swap = [remote(part(s_own, 1 - y, c), small(s_other, c), s_sem.at[c], s_sem_in.at[c], (partner, t)) for c in range(STATE_CHUNKS)]
    for c in range(STATE_CHUNKS):
        swap[c].start()
    reach = pairs // 2
    chain = [
        [remote(small(e_out.at[k], c), small(e_in.at[k], c), e_sem.at[k, c], e_sem_in.at[k, c], (s + 2, t)) for c in range(STATE_CHUNKS)]
        for k in range(reach)
    ]
    give = [remote(small(i_out, c), part(incoming, y, c), i_sem.at[c], i_sem_in.at[c], (partner, t)) for c in range(STATE_CHUNKS)]
    take = [remote(small(i_out, c), part(incoming, 1 - y, c), i_sem.at[c], i_sem_in.at[c], (partner, t)) for c in range(STATE_CHUNKS)]

    project_read(diagonal)
    grow = jnp.exp(cum)
    query = acc_q[...].astype(BF16).astype(F32)
    qdec = (query * grow * K ** -0.5).astype(BF16)
    kinv = (key * jnp.exp(-cum)).astype(BF16)
    from_prev = jnp.where(id_col[:, 0:1] == id_prev, 1.0, 0.0)

    def local_block(b):
        mine = slice(b * C, (b + 1) * C)
        seen = (b + 1) * C
        keys = [
            (kend[a] * jnp.exp(sum(totals[a + 1:b], zero))).astype(BF16) for a in range(b)
        ] + [kinv[mine]]
        scores = dot_nt(qdec[mine], jnp.concatenate(keys, axis=0))
        allowed = (col[mine, :seen] <= row[mine, :seen]) & (id_col[mine, :seen] == id_row[:, :seen])
        weights = jnp.where(allowed, scores, 0.0).astype(BF16)
        attn_ref[mine, :] = dot(weights, value[:seen])
        qin_ref[mine, :] = (
            qdec[mine].astype(F32) * jnp.exp(sum(totals[:b], zero)) * from_prev[mine]
        ).astype(BF16)

    for k in range(reach):
        @pl.when(g <= k)
        def _():
            e_in[k] = jnp.zeros_like(e_in[k])

    second = y.astype(F32)
    first = 1.0 - second
    send_p.wait_recv()
    own_decay, other_decay = p_own[0:1, :], p_other[0:1, :]
    p0 = own_decay * first + other_decay * second
    p1 = own_decay * second + other_decay * first
    both = p0 * p1

    def place(c):
        return pl.ds(pl.multiple_of(y * half + c * span, span), span)

    for c in range(STATE_CHUNKS):
        swap[c].wait_recv()
        mine = pl.ds(c * span, span)
        a, b = s_own[place(c), :].astype(F32), s_other[mine, :].astype(F32)
        s0 = a * first + b * second
        s1 = a * second + b * first
        pair_first[mine, :] = s0

        @pl.when(g < last)
        def _():
            e_out[0, mine, :] = (p1 * s0 + s1).astype(BF16)
            chain[0][c].start()

    local_block(0)
    local_block(1)
    for k in range(1, reach):
        for c in range(STATE_CHUNKS):
            mine = pl.ds(c * span, span)

            @pl.when(g >= k)
            def _():
                chain[k - 1][c].wait_recv()

            @pl.when((g >= k) & (g < last))
            def _():
                e_out[k, mine, :] = (both * e_in[k - 1, mine, :].astype(F32)).astype(BF16)
                chain[k][c].start()

    local_block(2)
    for c in range(STATE_CHUNKS):
        mine = pl.ds(c * span, span)

        @pl.when(g >= reach)
        def _():
            chain[reach - 1][c].wait_recv()

        entry = e_in[0, mine, :].astype(F32)
        for k in range(1, reach):
            entry += e_in[k, mine, :].astype(F32)
        middle_state = p0 * entry + pair_first[mine, :]
        i_out[mine, :] = (middle_state * first + entry * second).astype(BF16)
        give[c].start()
        incoming[place(c), :] = (entry * first + middle_state * second).astype(BF16)
    for b in range(3, blocks):
        local_block(b)
    opengate = acc_g[...]
    acc_g[...] = head_gain_ref[...] * (opengate * jax.nn.sigmoid(opengate))
    for load in loads[4:]:
        load.wait()
    for c in range(STATE_CHUNKS):
        take[c].wait_recv()

    lot = rows // OUT_CHUNKS

    def lines(c):
        return pl.ds(c * lot, lot)

    share = [
        [remote(mate_out.at[k, lines(c)], mate_in.at[k, lines(c)], m_sem.at[k, c], m_sem_in.at[k, c], (s, mate)) for c in range(OUT_CHUNKS)]
        for k in range(2)
    ]
    over = [remote(x_out.at[lines(c)], x_in.at[lines(c)], x_sem.at[c], x_sem_in.at[c], (s, across)) for c in range(OUT_CHUNKS)]
    attn_ref[...] += dot_nt(qin_ref[...], incoming[...])
    for c in range(OUT_CHUNKS):
        attn = attn_ref[lines(c), :]
        scale = lax.rsqrt(jnp.mean(attn * attn, axis=-1, keepdims=True) + 1e-5)
        gated_ref[lines(c), :] = (attn * scale * acc_g[lines(c), :]).astype(BF16)
        mate_out[0, lines(c), :] = dot(gated_ref[lines(c), :], wo[diagonal]).astype(BF16)
        share[0][c].start()
    for c in range(OUT_CHUNKS):
        keep_x = dot(gated_ref[lines(c), :], wo[across])
        share[0][c].wait_recv()
        x_out[lines(c), :] = (keep_x + mate_in[0, lines(c), :].astype(F32)).astype(BF16)
        over[c].start()
    for c in range(OUT_CHUNKS):
        mate_out[1, lines(c), :] = dot(gated_ref[lines(c), :], wo[mate]).astype(BF16)
        share[1][c].start()
        keep_own[lines(c), :] = dot(gated_ref[lines(c), :], wo[t])
    for c in range(OUT_CHUNKS):
        share[1][c].wait_recv()
        over[c].wait_recv()
        out_ref[lines(c), :] = (
            keep_own[lines(c), :] + mate_in[1, lines(c), :].astype(F32) + x_in[lines(c), :].astype(F32)
        ).astype(BF16)

    for copy in to_x + to_mate + forward + send_ssq + [send_p] + swap + give + share[0] + share[1] + over:
        copy.wait_send()

    @pl.when(s < 2 * pairs - 1)
    def _():
        send_id.wait_send()

    for k in range(reach):
        @pl.when((g >= k) & (g < last))
        def _():
            for c in range(STATE_CHUNKS):
                chain[k][c].wait_send()


def per_device(
    pairs,
    tokens, norm_gain, w_query, w_key, w_value, w_gate_out, gate_down, gate_up, gate_bias,
    head_gain, w_out, request_ids,
):
    rows, feats = tokens.shape
    ranks = gate_down.shape[1]
    vmem = pl.BlockSpec(memory_space=pltpu.VMEM)
    hbm = pl.BlockSpec(memory_space=pl.ANY)
    half = V // 2
    dma = pltpu.SemaphoreType.DMA
    scratch = [
        pltpu.VMEM((4, rows, feats), BF16),
        pltpu.VMEM((4, feats, K), BF16),
        pltpu.VMEM((4, feats, K), BF16),
        pltpu.VMEM((4, feats, V), BF16),
        pltpu.VMEM((4, feats, V), BF16),
        pltpu.VMEM((4, V, feats), BF16),
        pltpu.VMEM((rows, K), F32),
        pltpu.VMEM((rows, K), F32),
        pltpu.VMEM((rows, V), F32),
        pltpu.VMEM((rows, V), F32),
        pltpu.VMEM((rows, ranks), F32),
        pltpu.VMEM((4, 8, rows), F32),
        pltpu.VMEM((rows, V), F32),
        pltpu.VMEM((rows, K), BF16),
        pltpu.VMEM((rows, V), BF16),
        pltpu.VMEM((8, 128), F32),
        pltpu.VMEM((8, 128), F32),
        pltpu.VMEM((8, K), F32),
        pltpu.VMEM((8, K), F32),
        pltpu.VMEM((V, K), BF16),
        pltpu.VMEM((half, K), BF16),
        pltpu.VMEM((pairs // 2, half, K), BF16),
        pltpu.VMEM((pairs // 2, half, K), BF16),
        pltpu.VMEM((half, K), BF16),
        pltpu.VMEM((V, K), BF16),
        pltpu.VMEM((2, rows, feats), BF16),
        pltpu.VMEM((2, rows, feats), BF16),
        pltpu.VMEM((rows, feats), BF16),
        pltpu.VMEM((rows, feats), BF16),
        pltpu.VMEM((rows, feats), F32),
        pltpu.VMEM((half, K), F32),
        dma((8,)),
        dma,
        dma((TOKEN_CHUNKS,)), dma((TOKEN_CHUNKS,)),
        dma((TOKEN_CHUNKS,)), dma((TOKEN_CHUNKS,)),
        dma((TOKEN_CHUNKS,)), dma((TOKEN_CHUNKS,)),
        dma((2,)), dma((2,)),
        dma((STATE_CHUNKS,)), dma((STATE_CHUNKS,)),
        dma((pairs // 2, STATE_CHUNKS)), dma((pairs // 2, STATE_CHUNKS)),
        dma((STATE_CHUNKS,)), dma((STATE_CHUNKS,)),
        dma((2, OUT_CHUNKS)), dma((2, OUT_CHUNKS)),
        dma((OUT_CHUNKS,)), dma((OUT_CHUNKS,)),
        dma((3,)), dma((3,)),
    ]
    return pl.pallas_call(
        functools.partial(kernel, pairs),
        out_shape=jax.ShapeDtypeStruct((rows, feats), BF16),
        in_specs=[hbm, vmem, hbm, hbm, hbm, hbm, vmem, vmem, vmem, vmem, hbm, vmem],
        out_specs=vmem,
        scratch_shapes=scratch,
        compiler_params=pltpu.CompilerParams(
            collective_id=0, has_side_effects=True, vmem_limit_bytes=62 * 2**20),
        cost_estimate=pl.CostEstimate(flops=2_500_000_000, bytes_accessed=10_000_000, transcendentals=400_000),
        name="gla",
    )(
        tokens,
        norm_gain.reshape(4, 1, feats),
        w_query.reshape(4, feats, K),
        w_key.reshape(4, feats, K),
        w_value.reshape(4, feats, V),
        w_gate_out.reshape(4, feats, V),
        gate_down.T,
        gate_up,
        gate_bias.reshape(1, K),
        head_gain.reshape(1, V),
        w_out,
        request_ids.reshape(1, rows),
    )


def solution(mesh):
    return jax.shard_map(
        functools.partial(per_device, mesh.shape["seq"] // 2),
        mesh=mesh,
        in_specs=(
            P("seq", "tp"),
            P(),
            P(None, "tp"),
            P(None, "tp"),
            P(None, "tp"),
            P(None, "tp"),
            P(),
            P(None, "tp"),
            P("tp"),
            P("tp"),
            P("tp", None),
            P("seq"),
        ),
        out_specs=P("seq", "tp"),
        check_vma=False,
    )
```

```python
import functools

import jax
import jax.numpy as jnp
from jax import lax
from jax.experimental import pallas as pl
from jax.experimental.pallas import tpu as pltpu
from jax.sharding import PartitionSpec as P

K = 256
V = 512
C = 64
F32 = jnp.float32
BF16 = jnp.bfloat16
MESH = pl.DeviceIdType.MESH
TOKEN_CHUNKS = 4
STATE_CHUNKS = 4
OUT_CHUNKS = 2


def dot(a, b):
    return jnp.dot(a, b, preferred_element_type=F32)


def dot_nt(a, b):
    return lax.dot_general(a, b, (((1,), (1,)), ((), ())), preferred_element_type=F32)


def dot_tn(a, b):
    return lax.dot_general(a, b, (((0,), (0,)), ((), ())), preferred_element_type=F32)


def kernel(
    pairs,
    tokens_ref, gain_ref, wq_hbm, wk_hbm, wv_hbm, wg_hbm, down_ref, up_ref, bias_ref,
    head_gain_ref, wo_hbm, ids_ref,
    out_ref,
    tok, wq, wk, wv, wg, wo,
    acc_q, acc_k, acc_v, acc_g, acc_low, ssq_all,
    attn_ref, qin_ref, gated_ref,
    id_out, id_in, p_own, p_other,
    s_own, s_other, e_in, e_out, i_out, incoming,
    mate_out, mate_in, x_out, x_in, keep_own, pair_first,
    load_sem, tok_sem, tok_x, tok_x_in, tok_mate, tok_mate_in, tok_fwd, tok_fwd_in,
    id_sem, p_sem, s_sem, s_sem_in, e_sem, e_sem_in, i_sem, i_sem_in,
    m_sem, m_sem_in, x_sem, x_sem_in, ssq_sem, ssq_sem_in,
):
    s, t = lax.axis_index("seq"), lax.axis_index("tp")
    y, g = s % 2, s // 2
    rows, feats = tokens_ref.shape
    mate = t + 1 - 2 * (t % 2)
    across = (t + 2) % 4
    diagonal = (mate + 2) % 4
    partner = s + 1 - 2 * y
    last = pairs - 1

    def remote(src, dst, send, recv, where):
        return pltpu.make_async_remote_copy(
            src_ref=src, dst_ref=dst, send_sem=send, recv_sem=recv,
            device_id=where, device_id_type=MESH)

    own_tokens = pltpu.make_async_copy(tokens_ref, tok.at[t], tok_sem)
    own_tokens.start()
    loads = [
        pltpu.make_async_copy(src, dst, load_sem.at[i])
        for i, (src, dst) in enumerate([(wk_hbm, wk), (wv_hbm, wv), (wq_hbm, wq), (wg_hbm, wg)])
    ]
    loads += [
        pltpu.make_async_copy(wo_hbm.at[:, pl.ds(j * feats, feats)], wo.at[j], load_sem.at[4 + j])
        for j in range(4)
    ]
    for load in loads:
        load.start()

    barrier = pltpu.get_barrier_semaphore()
    up_g, down_g = (g + 1) % pairs, (g + last) % pairs
    skew = ((g + y * 2 - 1 + pairs) % pairs) * 2 + 1 - y
    for device in ((s, mate), (s, across), (s, diagonal), (partner, t), (up_g * 2 + y, t), (down_g * 2 + y, t), (skew, t)):
        pl.semaphore_signal(barrier, inc=1, device_id=device, device_id_type=MESH)
    id_row = ids_ref[...].astype(F32)
    id_last = id_row[:, rows - 1:rows]
    id_out[...] = jnp.broadcast_to(id_last, id_out.shape)
    acc_q[...] = jnp.zeros_like(acc_q)
    acc_k[...] = jnp.zeros_like(acc_k)
    acc_v[...] = jnp.zeros_like(acc_v)
    acc_g[...] = jnp.zeros_like(acc_g)
    acc_low[...] = jnp.zeros_like(acc_low)
    own_tokens.wait()
    own = tok[t].astype(F32)
    squares = jnp.sum(own * own, axis=-1, keepdims=True)
    ssq_all[0] = jnp.broadcast_to(squares, (rows, 128)).T[0:8]
    pl.semaphore_wait(barrier, 7)
    send_ssq = [
        remote(ssq_all.at[0], ssq_all.at[i + 1], ssq_sem.at[i], ssq_sem_in.at[i], (s, peer))
        for i, peer in enumerate((mate, across, diagonal))
    ]
    for copy in send_ssq:
        copy.start()

    size = rows // TOKEN_CHUNKS

    def piece(block, c):
        return tok.at[block, pl.ds(c * size, size)]

    to_x = [remote(piece(t, c), piece(t, c), tok_x.at[c], tok_x_in.at[c], (s, across)) for c in range(TOKEN_CHUNKS)]
    to_mate = [remote(piece(t, c), piece(t, c), tok_mate.at[c], tok_mate_in.at[c], (s, mate)) for c in range(TOKEN_CHUNKS)]
    from_x = [remote(piece(across, c), piece(across, c), tok_x.at[c], tok_x_in.at[c], (s, across)) for c in range(TOKEN_CHUNKS)]
    from_mate = [remote(piece(mate, c), piece(mate, c), tok_mate.at[c], tok_mate_in.at[c], (s, mate)) for c in range(TOKEN_CHUNKS)]
    forward = [remote(piece(across, c), piece(across, c), tok_fwd.at[c], tok_fwd_in.at[c], (s, mate)) for c in range(TOKEN_CHUNKS)]
    from_fwd = [remote(piece(diagonal, c), piece(diagonal, c), tok_fwd.at[c], tok_fwd_in.at[c], (s, mate)) for c in range(TOKEN_CHUNKS)]
    for c in range(TOKEN_CHUNKS):
        to_x[c].start()
        to_mate[c].start()

    send_id = remote(id_out, id_in, id_sem.at[0], id_sem.at[1], (s + 1, t))

    @pl.when(s < 2 * pairs - 1)
    def _():
        send_id.start()

    def normed(block):
        return (tok[block].astype(F32) * r * gain_ref[block]).astype(BF16)

    def project_state(block):
        xg = normed(block)
        acc_low[...] += dot_nt(xg, down_ref[:, pl.ds(pl.multiple_of(block * feats, feats), feats)])
        acc_k[...] += dot(xg, wk[block])
        acc_v[...] += dot(xg, wv[block])
        return xg

    def project_read(block, xg):
        acc_q[...] += dot(xg, wq[block])
        acc_g[...] += dot(xg, wg[block])

    for copy in send_ssq:
        copy.wait_recv()
    total = ssq_all[0] + ssq_all[1] + ssq_all[2] + ssq_all[3]
    scale_row = lax.rsqrt(total / (4 * feats) + 1e-5)[0:1]
    r = jnp.broadcast_to(scale_row, (128, rows)).T[:, 0:1]
    for load in loads[:4]:
        load.wait()
    project_read(t, project_state(t))
    from_x[0].wait_recv()
    forward[0].start()
    for c in range(TOKEN_CHUNKS):
        from_mate[c].wait_recv()
    project_read(mate, project_state(mate))
    for c in range(1, TOKEN_CHUNKS):
        from_x[c].wait_recv()
        forward[c].start()
    project_read(across, project_state(across))
    for c in range(TOKEN_CHUNKS):
        from_fwd[c].wait_recv()
    last_normed = project_state(diagonal)

    low = acc_low[...].astype(BF16)
    z = dot(low, up_ref[...]) + bias_ref[...]
    rate = (jnp.minimum(z, 0.0) - jnp.log1p(jnp.exp(-jnp.abs(z)))) / 16.0
    row = lax.broadcasted_iota(jnp.int32, (rows, rows), 0)
    col = lax.broadcasted_iota(jnp.int32, (rows, rows), 1)
    within = jnp.where((row // C == col // C) & (col <= row), 1.0, 0.0).astype(BF16)
    high = rate.astype(BF16)
    rest = rate - high.astype(F32)
    middle = rest.astype(BF16)
    tiny = (rest - middle.astype(F32)).astype(BF16)
    cum = dot(within, high) + dot(within, middle) + dot(within, tiny)
    blocks = rows // C
    totals = [cum[(b + 1) * C - 1:(b + 1) * C] for b in range(blocks)]
    id_col = jnp.broadcast_to(id_row, (rows, rows)).T

    @pl.when(s == 0)
    def _():
        id_in[...] = jnp.full_like(id_in, -1.0)

    @pl.when(s > 0)
    def _():
        send_id.wait_recv()

    id_prev = id_in[0:1, 0:1]
    key = acc_k[...].astype(BF16).astype(F32)
    value = acc_v[...].astype(BF16)
    keep = jnp.where(id_col[:, 0:1] == id_last, 1.0, 0.0)
    zero = jnp.zeros_like(totals[0])
    kend, kdev = [], []
    for b in range(blocks):
        mine = slice(b * C, (b + 1) * C)
        end = key[mine] * jnp.exp(totals[b] - cum[mine])
        kend.append(end)
        kdev.append((end * jnp.exp(sum(totals[b + 1:], zero)) * keep[mine]).astype(BF16))
    state = dot_tn(value, jnp.concatenate(kdev, axis=0))
    s_own[...] = state.astype(BF16)
    going_on = jnp.where(id_last == id_prev, 1.0, 0.0)
    p_own[...] = jnp.broadcast_to(jnp.exp(sum(totals, zero)) * going_on, p_own.shape)

    half = V // 2
    span = half // STATE_CHUNKS

    def part(ref, owner, c):
        return ref.at[pl.ds(pl.multiple_of(owner * half + c * span, span), span)]

    def small(ref, c):
        return ref.at[pl.ds(c * span, span)]

    send_p = remote(p_own, p_other, p_sem.at[0], p_sem.at[1], (partner, t))
    send_p.start()
    swap = [remote(part(s_own, 1 - y, c), small(s_other, c), s_sem.at[c], s_sem_in.at[c], (partner, t)) for c in range(STATE_CHUNKS)]
    for c in range(STATE_CHUNKS):
        swap[c].start()
    reach = pairs // 2
    chain = [
        [remote(small(e_out.at[k], c), small(e_in.at[k], c), e_sem.at[k, c], e_sem_in.at[k, c], (s + 2, t)) for c in range(STATE_CHUNKS)]
        for k in range(reach)
    ]
    give = [remote(small(i_out, c), part(incoming, y, c), i_sem.at[c], i_sem_in.at[c], (partner, t)) for c in range(STATE_CHUNKS)]
    take = [remote(small(i_out, c), part(incoming, 1 - y, c), i_sem.at[c], i_sem_in.at[c], (partner, t)) for c in range(STATE_CHUNKS)]

    project_read(diagonal, last_normed)
    grow = jnp.exp(cum)
    query = acc_q[...].astype(BF16).astype(F32)
    qdec = (query * grow * K ** -0.5).astype(BF16)
    kinv = (key * jnp.exp(-cum)).astype(BF16)
    from_prev = jnp.where(id_col[:, 0:1] == id_prev, 1.0, 0.0)

    def local_block(b):
        mine = slice(b * C, (b + 1) * C)
        seen = (b + 1) * C
        keys = [
            (kend[a] * jnp.exp(sum(totals[a + 1:b], zero))).astype(BF16) for a in range(b)
        ] + [kinv[mine]]
        scores = dot_nt(qdec[mine], jnp.concatenate(keys, axis=0))
        allowed = (col[mine, :seen] <= row[mine, :seen]) & (id_col[mine, :seen] == id_row[:, :seen])
        weights = jnp.where(allowed, scores, 0.0).astype(BF16)
        attn_ref[mine, :] = dot(weights, value[:seen])
        qin_ref[mine, :] = (
            qdec[mine].astype(F32) * jnp.exp(sum(totals[:b], zero)) * from_prev[mine]
        ).astype(BF16)

    for k in range(reach):
        @pl.when(g <= k)
        def _():
            e_in[k] = jnp.zeros_like(e_in[k])

    second = y.astype(F32)
    first = 1.0 - second
    send_p.wait_recv()
    own_decay, other_decay = p_own[0:1, :], p_other[0:1, :]
    p0 = own_decay * first + other_decay * second
    p1 = own_decay * second + other_decay * first
    both = p0 * p1

    def place(c):
        return pl.ds(pl.multiple_of(y * half + c * span, span), span)

    for c in range(STATE_CHUNKS):
        swap[c].wait_recv()
        mine = pl.ds(c * span, span)
        a, b = s_own[place(c), :].astype(F32), s_other[mine, :].astype(F32)
        s0 = a * first + b * second
        s1 = a * second + b * first
        pair_first[mine, :] = s0

        @pl.when(g < last)
        def _():
            e_out[0, mine, :] = (p1 * s0 + s1).astype(BF16)
            chain[0][c].start()

    local_block(0)
    local_block(1)
    for k in range(1, reach):
        for c in range(STATE_CHUNKS):
            mine = pl.ds(c * span, span)

            @pl.when(g >= k)
            def _():
                chain[k - 1][c].wait_recv()

            @pl.when((g >= k) & (g < last))
            def _():
                e_out[k, mine, :] = (both * e_in[k - 1, mine, :].astype(F32)).astype(BF16)
                chain[k][c].start()

    local_block(2)
    for c in range(STATE_CHUNKS):
        mine = pl.ds(c * span, span)

        @pl.when(g >= reach)
        def _():
            chain[reach - 1][c].wait_recv()

        entry = e_in[0, mine, :].astype(F32)
        for k in range(1, reach):
            entry += e_in[k, mine, :].astype(F32)
        middle_state = p0 * entry + pair_first[mine, :]
        i_out[mine, :] = (middle_state * first + entry * second).astype(BF16)
        give[c].start()
        incoming[place(c), :] = (entry * first + middle_state * second).astype(BF16)
    for b in range(3, blocks):
        local_block(b)
    opengate = acc_g[...]
    acc_g[...] = head_gain_ref[...] * (opengate * jax.nn.sigmoid(opengate))
    for load in loads[4:]:
        load.wait()
    for c in range(STATE_CHUNKS):
        take[c].wait_recv()

    lot = rows // OUT_CHUNKS

    def lines(c):
        return pl.ds(c * lot, lot)

    share = [
        [remote(mate_out.at[k, lines(c)], mate_in.at[k, lines(c)], m_sem.at[k, c], m_sem_in.at[k, c], (s, mate)) for c in range(OUT_CHUNKS)]
        for k in range(2)
    ]
    over = [remote(x_out.at[lines(c)], x_in.at[lines(c)], x_sem.at[c], x_sem_in.at[c], (s, across)) for c in range(OUT_CHUNKS)]
    attn_ref[...] += dot_nt(qin_ref[...], incoming[...])
    for c in range(OUT_CHUNKS):
        attn = attn_ref[lines(c), :]
        scale = lax.rsqrt(jnp.mean(attn * attn, axis=-1, keepdims=True) + 1e-5)
        gated_ref[lines(c), :] = (attn * scale * acc_g[lines(c), :]).astype(BF16)
        mate_out[0, lines(c), :] = dot(gated_ref[lines(c), :], wo[diagonal]).astype(BF16)
        share[0][c].start()
    for c in range(OUT_CHUNKS):
        keep_x = dot(gated_ref[lines(c), :], wo[across])
        share[0][c].wait_recv()
        x_out[lines(c), :] = (keep_x + mate_in[0, lines(c), :].astype(F32)).astype(BF16)
        over[c].start()
    for c in range(OUT_CHUNKS):
        mate_out[1, lines(c), :] = dot(gated_ref[lines(c), :], wo[mate]).astype(BF16)
        share[1][c].start()
        keep_own[lines(c), :] = dot(gated_ref[lines(c), :], wo[t])
    for c in range(OUT_CHUNKS):
        share[1][c].wait_recv()
        over[c].wait_recv()
        out_ref[lines(c), :] = (
            keep_own[lines(c), :] + mate_in[1, lines(c), :].astype(F32) + x_in[lines(c), :].astype(F32)
        ).astype(BF16)

    for copy in to_x + to_mate + forward + send_ssq + [send_p] + swap + give + share[0] + share[1] + over:
        copy.wait_send()

    @pl.when(s < 2 * pairs - 1)
    def _():
        send_id.wait_send()

    for k in range(reach):
        @pl.when((g >= k) & (g < last))
        def _():
            for c in range(STATE_CHUNKS):
                chain[k][c].wait_send()


def per_device(
    pairs,
    tokens, norm_gain, w_query, w_key, w_value, w_gate_out, gate_down, gate_up, gate_bias,
    head_gain, w_out, request_ids,
):
    rows, feats = tokens.shape
    ranks = gate_down.shape[1]
    vmem = pl.BlockSpec(memory_space=pltpu.VMEM)
    hbm = pl.BlockSpec(memory_space=pl.ANY)
    half = V // 2
    dma = pltpu.SemaphoreType.DMA
    scratch = [
        pltpu.VMEM((4, rows, feats), BF16),
        pltpu.VMEM((4, feats, K), BF16),
        pltpu.VMEM((4, feats, K), BF16),
        pltpu.VMEM((4, feats, V), BF16),
        pltpu.VMEM((4, feats, V), BF16),
        pltpu.VMEM((4, V, feats), BF16),
        pltpu.VMEM((rows, K), F32),
        pltpu.VMEM((rows, K), F32),
        pltpu.VMEM((rows, V), F32),
        pltpu.VMEM((rows, V), F32),
        pltpu.VMEM((rows, ranks), F32),
        pltpu.VMEM((4, 8, rows), F32),
        pltpu.VMEM((rows, V), F32),
        pltpu.VMEM((rows, K), BF16),
        pltpu.VMEM((rows, V), BF16),
        pltpu.VMEM((8, 128), F32),
        pltpu.VMEM((8, 128), F32),
        pltpu.VMEM((8, K), F32),
        pltpu.VMEM((8, K), F32),
        pltpu.VMEM((V, K), BF16),
        pltpu.VMEM((half, K), BF16),
        pltpu.VMEM((pairs // 2, half, K), BF16),
        pltpu.VMEM((pairs // 2, half, K), BF16),
        pltpu.VMEM((half, K), BF16),
        pltpu.VMEM((V, K), BF16),
        pltpu.VMEM((2, rows, feats), BF16),
        pltpu.VMEM((2, rows, feats), BF16),
        pltpu.VMEM((rows, feats), BF16),
        pltpu.VMEM((rows, feats), BF16),
        pltpu.VMEM((rows, feats), F32),
        pltpu.VMEM((half, K), F32),
        dma((8,)),
        dma,
        dma((TOKEN_CHUNKS,)), dma((TOKEN_CHUNKS,)),
        dma((TOKEN_CHUNKS,)), dma((TOKEN_CHUNKS,)),
        dma((TOKEN_CHUNKS,)), dma((TOKEN_CHUNKS,)),
        dma((2,)), dma((2,)),
        dma((STATE_CHUNKS,)), dma((STATE_CHUNKS,)),
        dma((pairs // 2, STATE_CHUNKS)), dma((pairs // 2, STATE_CHUNKS)),
        dma((STATE_CHUNKS,)), dma((STATE_CHUNKS,)),
        dma((2, OUT_CHUNKS)), dma((2, OUT_CHUNKS)),
        dma((OUT_CHUNKS,)), dma((OUT_CHUNKS,)),
        dma((3,)), dma((3,)),
    ]
    return pl.pallas_call(
        functools.partial(kernel, pairs),
        out_shape=jax.ShapeDtypeStruct((rows, feats), BF16),
        in_specs=[hbm, vmem, hbm, hbm, hbm, hbm, vmem, vmem, vmem, vmem, hbm, vmem],
        out_specs=vmem,
        scratch_shapes=scratch,
        compiler_params=pltpu.CompilerParams(
            collective_id=0, has_side_effects=True, vmem_limit_bytes=62 * 2**20),
        cost_estimate=pl.CostEstimate(flops=2_500_000_000, bytes_accessed=10_000_000, transcendentals=400_000),
        name="gla",
    )(
        tokens,
        norm_gain.reshape(4, 1, feats),
        w_query.reshape(4, feats, K),
        w_key.reshape(4, feats, K),
        w_value.reshape(4, feats, V),
        w_gate_out.reshape(4, feats, V),
        gate_down.T,
        gate_up,
        gate_bias.reshape(1, K),
        head_gain.reshape(1, V),
        w_out,
        request_ids.reshape(1, rows),
    )


def solution(mesh):
    return jax.shard_map(
        functools.partial(per_device, mesh.shape["seq"] // 2),
        mesh=mesh,
        in_specs=(
            P("seq", "tp"),
            P(),
            P(None, "tp"),
            P(None, "tp"),
            P(None, "tp"),
            P(None, "tp"),
            P(),
            P(None, "tp"),
            P("tp"),
            P("tp"),
            P("tp", None),
            P("seq"),
        ),
        out_specs=P("seq", "tp"),
        check_vma=False,
    )
```

```python
import functools

import jax
import jax.numpy as jnp
from jax import lax
from jax.experimental import pallas as pl
from jax.experimental.pallas import tpu as pltpu
from jax.sharding import PartitionSpec as P

K = 256
V = 512
C = 64
F32 = jnp.float32
BF16 = jnp.bfloat16
MESH = pl.DeviceIdType.MESH
TOKEN_CHUNKS = 4
STATE_CHUNKS = 4
OUT_CHUNKS = 2


def dot(a, b):
    return jnp.dot(a, b, preferred_element_type=F32)


def dot_nt(a, b):
    return lax.dot_general(a, b, (((1,), (1,)), ((), ())), preferred_element_type=F32)


def dot_tn(a, b):
    return lax.dot_general(a, b, (((0,), (0,)), ((), ())), preferred_element_type=F32)


def kernel(
    pairs,
    tokens_ref, gain_ref, wq_hbm, wk_hbm, wv_hbm, wg_hbm, down_ref, up_ref, bias_ref,
    head_gain_ref, wo_hbm, ids_ref,
    out_ref,
    tok, wq, wk, wv, wg, wo,
    acc_q, acc_k, acc_v, acc_g, acc_low, ssq_all,
    attn_ref, qin_ref, gated_ref,
    id_out, id_in, p_own, p_other,
    s_own, s_other, e_in, e_out, i_out, incoming,
    mate_out, mate_in, x_out, x_in, keep_own, pair_first,
    load_sem, tok_sem, tok_x, tok_x_in, tok_mate, tok_mate_in, tok_fwd, tok_fwd_in,
    id_sem, p_sem, s_sem, s_sem_in, e_sem, e_sem_in, i_sem, i_sem_in,
    m_sem, m_sem_in, x_sem, x_sem_in, ssq_sem, ssq_sem_in,
):
    s, t = lax.axis_index("seq"), lax.axis_index("tp")
    y, g = s % 2, s // 2
    rows, feats = tokens_ref.shape
    mate = t + 1 - 2 * (t % 2)
    across = (t + 2) % 4
    diagonal = (mate + 2) % 4
    partner = s + 1 - 2 * y
    last = pairs - 1

    def remote(src, dst, send, recv, where):
        return pltpu.make_async_remote_copy(
            src_ref=src, dst_ref=dst, send_sem=send, recv_sem=recv,
            device_id=where, device_id_type=MESH)

    own_tokens = pltpu.make_async_copy(tokens_ref, tok.at[t], tok_sem)
    own_tokens.start()
    loads = [
        pltpu.make_async_copy(src, dst, load_sem.at[i])
        for i, (src, dst) in enumerate([(wk_hbm, wk), (wv_hbm, wv), (wq_hbm, wq), (wg_hbm, wg)])
    ]
    loads += [
        pltpu.make_async_copy(wo_hbm.at[:, pl.ds(j * feats, feats)], wo.at[j], load_sem.at[4 + j])
        for j in range(4)
    ]
    for load in loads:
        load.start()

    barrier = pltpu.get_barrier_semaphore()
    up_g, down_g = (g + 1) % pairs, (g + last) % pairs
    skew = ((g + y * 2 - 1 + pairs) % pairs) * 2 + 1 - y
    for device in ((s, mate), (s, across), (s, diagonal), (partner, t), (up_g * 2 + y, t), (down_g * 2 + y, t), (skew, t)):
        pl.semaphore_signal(barrier, inc=1, device_id=device, device_id_type=MESH)
    id_row = ids_ref[...].astype(F32)
    id_last = id_row[:, rows - 1:rows]
    id_out[...] = jnp.broadcast_to(id_last, id_out.shape)
    acc_q[...] = jnp.zeros_like(acc_q)
    acc_k[...] = jnp.zeros_like(acc_k)
    acc_v[...] = jnp.zeros_like(acc_v)
    acc_g[...] = jnp.zeros_like(acc_g)
    acc_low[...] = jnp.zeros_like(acc_low)
    own_tokens.wait()
    own = tok[t].astype(F32)
    squares = jnp.sum(own * own, axis=-1, keepdims=True)
    ssq_all[0] = jnp.broadcast_to(squares, (rows, 128)).T[0:8]
    pl.semaphore_wait(barrier, 7)
    send_ssq = [
        remote(ssq_all.at[0], ssq_all.at[i + 1], ssq_sem.at[i], ssq_sem_in.at[i], (s, peer))
        for i, peer in enumerate((mate, across, diagonal))
    ]
    for copy in send_ssq:
        copy.start()

    size = rows // TOKEN_CHUNKS

    def piece(block, c):
        return tok.at[block, pl.ds(c * size, size)]

    to_x = [remote(piece(t, c), piece(t, c), tok_x.at[c], tok_x_in.at[c], (s, across)) for c in range(TOKEN_CHUNKS)]
    to_mate = [remote(piece(t, c), piece(t, c), tok_mate.at[c], tok_mate_in.at[c], (s, mate)) for c in range(TOKEN_CHUNKS)]
    from_x = [remote(piece(across, c), piece(across, c), tok_x.at[c], tok_x_in.at[c], (s, across)) for c in range(TOKEN_CHUNKS)]
    from_mate = [remote(piece(mate, c), piece(mate, c), tok_mate.at[c], tok_mate_in.at[c], (s, mate)) for c in range(TOKEN_CHUNKS)]
    forward = [remote(piece(across, c), piece(across, c), tok_fwd.at[c], tok_fwd_in.at[c], (s, mate)) for c in range(TOKEN_CHUNKS)]
    from_fwd = [remote(piece(diagonal, c), piece(diagonal, c), tok_fwd.at[c], tok_fwd_in.at[c], (s, mate)) for c in range(TOKEN_CHUNKS)]
    for c in range(TOKEN_CHUNKS):
        to_x[c].start()
        to_mate[c].start()

    send_id = remote(id_out, id_in, id_sem.at[0], id_sem.at[1], (s + 1, t))

    @pl.when(s < 2 * pairs - 1)
    def _():
        send_id.start()

    def normed(block):
        return (tok[block].astype(F32) * r * gain_ref[block]).astype(BF16)

    def project_state(block):
        xg = normed(block)
        acc_low[...] += dot_nt(xg, down_ref[:, pl.ds(pl.multiple_of(block * feats, feats), feats)])
        acc_k[...] += dot(xg, wk[block])
        acc_v[...] += dot(xg, wv[block])
        return xg

    def project_read(block, xg):
        acc_q[...] += dot(xg, wq[block])
        acc_g[...] += dot(xg, wg[block])

    for copy in send_ssq:
        copy.wait_recv()
    total = ssq_all[0] + ssq_all[1] + ssq_all[2] + ssq_all[3]
    scale_row = lax.rsqrt(total / (4 * feats) + 1e-5)[0:1]
    r = jnp.broadcast_to(scale_row, (128, rows)).T[:, 0:1]
    for load in loads[:4]:
        load.wait()
    project_read(t, project_state(t))
    from_x[0].wait_recv()
    forward[0].start()
    for c in range(TOKEN_CHUNKS):
        from_mate[c].wait_recv()
    project_read(mate, project_state(mate))
    for c in range(1, TOKEN_CHUNKS):
        from_x[c].wait_recv()
        forward[c].start()
    across_normed = project_state(across)
    for c in range(TOKEN_CHUNKS):
        from_fwd[c].wait_recv()
    last_normed = project_state(diagonal)

    low = acc_low[...].astype(BF16)
    z = dot(low, up_ref[...]) + bias_ref[...]
    rate = (jnp.minimum(z, 0.0) - jnp.log1p(jnp.exp(-jnp.abs(z)))) / 16.0
    row = lax.broadcasted_iota(jnp.int32, (rows, rows), 0)
    col = lax.broadcasted_iota(jnp.int32, (rows, rows), 1)
    within = jnp.where((row // C == col // C) & (col <= row), 1.0, 0.0).astype(BF16)
    high = rate.astype(BF16)
    rest = rate - high.astype(F32)
    middle = rest.astype(BF16)
    tiny = (rest - middle.astype(F32)).astype(BF16)
    cum = dot(within, high) + dot(within, middle) + dot(within, tiny)
    blocks = rows // C
    totals = [cum[(b + 1) * C - 1:(b + 1) * C] for b in range(blocks)]
    id_col = jnp.broadcast_to(id_row, (rows, rows)).T

    @pl.when(s == 0)
    def _():
        id_in[...] = jnp.full_like(id_in, -1.0)

    @pl.when(s > 0)
    def _():
        send_id.wait_recv()

    id_prev = id_in[0:1, 0:1]
    key = acc_k[...].astype(BF16).astype(F32)
    value = acc_v[...].astype(BF16)
    keep = jnp.where(id_col[:, 0:1] == id_last, 1.0, 0.0)
    zero = jnp.zeros_like(totals[0])
    kend, kdev = [], []
    for b in range(blocks):
        mine = slice(b * C, (b + 1) * C)
        end = key[mine] * jnp.exp(totals[b] - cum[mine])
        kend.append(end)
        kdev.append((end * jnp.exp(sum(totals[b + 1:], zero)) * keep[mine]).astype(BF16))
    state = dot_tn(value, jnp.concatenate(kdev, axis=0))
    s_own[...] = state.astype(BF16)
    going_on = jnp.where(id_last == id_prev, 1.0, 0.0)
    p_own[...] = jnp.broadcast_to(jnp.exp(sum(totals, zero)) * going_on, p_own.shape)

    half = V // 2
    span = half // STATE_CHUNKS

    def part(ref, owner, c):
        return ref.at[pl.ds(pl.multiple_of(owner * half + c * span, span), span)]

    def small(ref, c):
        return ref.at[pl.ds(c * span, span)]

    send_p = remote(p_own, p_other, p_sem.at[0], p_sem.at[1], (partner, t))
    send_p.start()
    swap = [remote(part(s_own, 1 - y, c), small(s_other, c), s_sem.at[c], s_sem_in.at[c], (partner, t)) for c in range(STATE_CHUNKS)]
    for c in range(STATE_CHUNKS):
        swap[c].start()
    reach = pairs // 2
    chain = [
        [remote(small(e_out.at[k], c), small(e_in.at[k], c), e_sem.at[k, c], e_sem_in.at[k, c], (s + 2, t)) for c in range(STATE_CHUNKS)]
        for k in range(reach)
    ]
    give = [remote(small(i_out, c), part(incoming, y, c), i_sem.at[c], i_sem_in.at[c], (partner, t)) for c in range(STATE_CHUNKS)]
    take = [remote(small(i_out, c), part(incoming, 1 - y, c), i_sem.at[c], i_sem_in.at[c], (partner, t)) for c in range(STATE_CHUNKS)]

    project_read(across, across_normed)
    project_read(diagonal, last_normed)
    grow = jnp.exp(cum)
    query = acc_q[...].astype(BF16).astype(F32)
    qdec = (query * grow * K ** -0.5).astype(BF16)
    kinv = (key * jnp.exp(-cum)).astype(BF16)
    from_prev = jnp.where(id_col[:, 0:1] == id_prev, 1.0, 0.0)

    def local_block(b):
        mine = slice(b * C, (b + 1) * C)
        seen = (b + 1) * C
        keys = [
            (kend[a] * jnp.exp(sum(totals[a + 1:b], zero))).astype(BF16) for a in range(b)
        ] + [kinv[mine]]
        scores = dot_nt(qdec[mine], jnp.concatenate(keys, axis=0))
        allowed = (col[mine, :seen] <= row[mine, :seen]) & (id_col[mine, :seen] == id_row[:, :seen])
        weights = jnp.where(allowed, scores, 0.0).astype(BF16)
        attn_ref[mine, :] = dot(weights, value[:seen])
        qin_ref[mine, :] = (
            qdec[mine].astype(F32) * jnp.exp(sum(totals[:b], zero)) * from_prev[mine]
        ).astype(BF16)

    for k in range(reach):
        @pl.when(g <= k)
        def _():
            e_in[k] = jnp.zeros_like(e_in[k])

    second = y.astype(F32)
    first = 1.0 - second
    send_p.wait_recv()
    own_decay, other_decay = p_own[0:1, :], p_other[0:1, :]
    p0 = own_decay * first + other_decay * second
    p1 = own_decay * second + other_decay * first
    both = p0 * p1

    def place(c):
        return pl.ds(pl.multiple_of(y * half + c * span, span), span)

    for c in range(STATE_CHUNKS):
        swap[c].wait_recv()
        mine = pl.ds(c * span, span)
        a, b = s_own[place(c), :].astype(F32), s_other[mine, :].astype(F32)
        s0 = a * first + b * second
        s1 = a * second + b * first
        pair_first[mine, :] = s0

        @pl.when(g < last)
        def _():
            e_out[0, mine, :] = (p1 * s0 + s1).astype(BF16)
            chain[0][c].start()

    local_block(0)
    local_block(1)
    for k in range(1, reach):
        for c in range(STATE_CHUNKS):
            mine = pl.ds(c * span, span)

            @pl.when(g >= k)
            def _():
                chain[k - 1][c].wait_recv()

            @pl.when((g >= k) & (g < last))
            def _():
                e_out[k, mine, :] = (both * e_in[k - 1, mine, :].astype(F32)).astype(BF16)
                chain[k][c].start()

    local_block(2)
    for c in range(STATE_CHUNKS):
        mine = pl.ds(c * span, span)

        @pl.when(g >= reach)
        def _():
            chain[reach - 1][c].wait_recv()

        entry = e_in[0, mine, :].astype(F32)
        for k in range(1, reach):
            entry += e_in[k, mine, :].astype(F32)
        middle_state = p0 * entry + pair_first[mine, :]
        i_out[mine, :] = (middle_state * first + entry * second).astype(BF16)
        give[c].start()
        incoming[place(c), :] = (entry * first + middle_state * second).astype(BF16)
    for b in range(3, blocks):
        local_block(b)
    opengate = acc_g[...]
    acc_g[...] = head_gain_ref[...] * (opengate * jax.nn.sigmoid(opengate))
    for load in loads[4:]:
        load.wait()
    for c in range(STATE_CHUNKS):
        take[c].wait_recv()

    lot = rows // OUT_CHUNKS

    def lines(c):
        return pl.ds(c * lot, lot)

    share = [
        [remote(mate_out.at[k, lines(c)], mate_in.at[k, lines(c)], m_sem.at[k, c], m_sem_in.at[k, c], (s, mate)) for c in range(OUT_CHUNKS)]
        for k in range(2)
    ]
    over = [remote(x_out.at[lines(c)], x_in.at[lines(c)], x_sem.at[c], x_sem_in.at[c], (s, across)) for c in range(OUT_CHUNKS)]
    attn_ref[...] += dot_nt(qin_ref[...], incoming[...])
    for c in range(OUT_CHUNKS):
        attn = attn_ref[lines(c), :]
        scale = lax.rsqrt(jnp.mean(attn * attn, axis=-1, keepdims=True) + 1e-5)
        gated_ref[lines(c), :] = (attn * scale * acc_g[lines(c), :]).astype(BF16)
        mate_out[0, lines(c), :] = dot(gated_ref[lines(c), :], wo[diagonal]).astype(BF16)
        share[0][c].start()
    for c in range(OUT_CHUNKS):
        keep_x = dot(gated_ref[lines(c), :], wo[across])
        share[0][c].wait_recv()
        x_out[lines(c), :] = (keep_x + mate_in[0, lines(c), :].astype(F32)).astype(BF16)
        over[c].start()
    for c in range(OUT_CHUNKS):
        mate_out[1, lines(c), :] = dot(gated_ref[lines(c), :], wo[mate]).astype(BF16)
        share[1][c].start()
        keep_own[lines(c), :] = dot(gated_ref[lines(c), :], wo[t])
    for c in range(OUT_CHUNKS):
        share[1][c].wait_recv()
        over[c].wait_recv()
        out_ref[lines(c), :] = (
            keep_own[lines(c), :] + mate_in[1, lines(c), :].astype(F32) + x_in[lines(c), :].astype(F32)
        ).astype(BF16)

    for copy in to_x + to_mate + forward + send_ssq + [send_p] + swap + give + share[0] + share[1] + over:
        copy.wait_send()

    @pl.when(s < 2 * pairs - 1)
    def _():
        send_id.wait_send()

    for k in range(reach):
        @pl.when((g >= k) & (g < last))
        def _():
            for c in range(STATE_CHUNKS):
                chain[k][c].wait_send()


def per_device(
    pairs,
    tokens, norm_gain, w_query, w_key, w_value, w_gate_out, gate_down, gate_up, gate_bias,
    head_gain, w_out, request_ids,
):
    rows, feats = tokens.shape
    ranks = gate_down.shape[1]
    vmem = pl.BlockSpec(memory_space=pltpu.VMEM)
    hbm = pl.BlockSpec(memory_space=pl.ANY)
    half = V // 2
    dma = pltpu.SemaphoreType.DMA
    scratch = [
        pltpu.VMEM((4, rows, feats), BF16),
        pltpu.VMEM((4, feats, K), BF16),
        pltpu.VMEM((4, feats, K), BF16),
        pltpu.VMEM((4, feats, V), BF16),
        pltpu.VMEM((4, feats, V), BF16),
        pltpu.VMEM((4, V, feats), BF16),
        pltpu.VMEM((rows, K), F32),
        pltpu.VMEM((rows, K), F32),
        pltpu.VMEM((rows, V), F32),
        pltpu.VMEM((rows, V), F32),
        pltpu.VMEM((rows, ranks), F32),
        pltpu.VMEM((4, 8, rows), F32),
        pltpu.VMEM((rows, V), F32),
        pltpu.VMEM((rows, K), BF16),
        pltpu.VMEM((rows, V), BF16),
        pltpu.VMEM((8, 128), F32),
        pltpu.VMEM((8, 128), F32),
        pltpu.VMEM((8, K), F32),
        pltpu.VMEM((8, K), F32),
        pltpu.VMEM((V, K), BF16),
        pltpu.VMEM((half, K), BF16),
        pltpu.VMEM((pairs // 2, half, K), BF16),
        pltpu.VMEM((pairs // 2, half, K), BF16),
        pltpu.VMEM((half, K), BF16),
        pltpu.VMEM((V, K), BF16),
        pltpu.VMEM((2, rows, feats), BF16),
        pltpu.VMEM((2, rows, feats), BF16),
        pltpu.VMEM((rows, feats), BF16),
        pltpu.VMEM((rows, feats), BF16),
        pltpu.VMEM((rows, feats), F32),
        pltpu.VMEM((half, K), F32),
        dma((8,)),
        dma,
        dma((TOKEN_CHUNKS,)), dma((TOKEN_CHUNKS,)),
        dma((TOKEN_CHUNKS,)), dma((TOKEN_CHUNKS,)),
        dma((TOKEN_CHUNKS,)), dma((TOKEN_CHUNKS,)),
        dma((2,)), dma((2,)),
        dma((STATE_CHUNKS,)), dma((STATE_CHUNKS,)),
        dma((pairs // 2, STATE_CHUNKS)), dma((pairs // 2, STATE_CHUNKS)),
        dma((STATE_CHUNKS,)), dma((STATE_CHUNKS,)),
        dma((2, OUT_CHUNKS)), dma((2, OUT_CHUNKS)),
        dma((OUT_CHUNKS,)), dma((OUT_CHUNKS,)),
        dma((3,)), dma((3,)),
    ]
    return pl.pallas_call(
        functools.partial(kernel, pairs),
        out_shape=jax.ShapeDtypeStruct((rows, feats), BF16),
        in_specs=[hbm, vmem, hbm, hbm, hbm, hbm, vmem, vmem, vmem, vmem, hbm, vmem],
        out_specs=vmem,
        scratch_shapes=scratch,
        compiler_params=pltpu.CompilerParams(
            collective_id=0, has_side_effects=True, vmem_limit_bytes=62 * 2**20),
        cost_estimate=pl.CostEstimate(flops=2_500_000_000, bytes_accessed=10_000_000, transcendentals=400_000),
        name="gla",
    )(
        tokens,
        norm_gain.reshape(4, 1, feats),
        w_query.reshape(4, feats, K),
        w_key.reshape(4, feats, K),
        w_value.reshape(4, feats, V),
        w_gate_out.reshape(4, feats, V),
        gate_down.T,
        gate_up,
        gate_bias.reshape(1, K),
        head_gain.reshape(1, V),
        w_out,
        request_ids.reshape(1, rows),
    )


def solution(mesh):
    return jax.shard_map(
        functools.partial(per_device, mesh.shape["seq"] // 2),
        mesh=mesh,
        in_specs=(
            P("seq", "tp"),
            P(),
            P(None, "tp"),
            P(None, "tp"),
            P(None, "tp"),
            P(None, "tp"),
            P(),
            P(None, "tp"),
            P("tp"),
            P("tp"),
            P("tp", None),
            P("seq"),
        ),
        out_specs=P("seq", "tp"),
        check_vma=False,
    )
```
